32 devices in a mesh: ctx: 8 (over z, y), tp: 4 (over x, core).
Axes of the slice: x: 2, y: 2, z: 4, core: 2. Of those that a mesh axis runs over, the one named last changes fastest.
Arguments:
- queries: bfloat16 [1024, 4096], P('ctx', 'tp'), may hold values from -64 to 64
- keys: bfloat16 [1024, 1024], P('ctx', 'tp'), may hold values from -4 to 4
- values: bfloat16 [1024, 1024], P('ctx', 'tp'), may hold values from -6 to 6
- grad_out: bfloat16 [1024, 4096], P('ctx', 'tp'), may hold values from -6 to 6
- out_weight: bfloat16 [4096, 4096], P(None, 'tp'), may hold values from -0.09375 to 0.09375
- segments: int32 [1024], P('ctx'), may hold values from 0 to 1, as said below
Outputs:
- query_grad: bfloat16 [1024, 4096], P('ctx', 'tp')
- key_gradient: bfloat16 [1024, 1024], P('ctx', 'tp')
- value_gradient: bfloat16 [1024, 1024], P('ctx', 'tp')
The draws below stay inside these ranges and needn't reach their ends.
Inputs may be any that keep to these rules, and one draw needn't show every extreme that they name: `segments`: document numbers never fall along the tokens, start at 0, and every document starts at a multiple of 8 tokens; there are exactly 2 documents.
All inputs are finite; a program needn't handle non-finite values.
Results may differ from the reference program's by a relative error of at most 0.015.
Values may be sent and summed in bfloat16 or wider, within the bound.
A program may use at most 128 MiB of HBM per device.

```python
import jax
import jax.numpy as jnp
from jax import lax

D = 4096
QUERY_HEADS = 32
KEY_VALUE_HEADS = 8
HEAD_SIZE = 128
DOCS = 2
SEQUENCE_TOKENS = 1024


def draw_keys(key, part):
    owned_part = jax.random.fold_in(key, 3)
    final_result = jnp.clip(jax.random.normal(owned_part, (SEQUENCE_TOKENS, KEY_VALUE_HEADS * HEAD_SIZE), jnp.float32), -4.0, 4.0)
    return final_result.astype(jnp.bfloat16)


def draw_queries(key, part):
    owned_part = jax.random.fold_in(key, 5)
    final_result = jnp.clip(jax.random.normal(owned_part, (SEQUENCE_TOKENS, QUERY_HEADS * HEAD_SIZE), jnp.float32), -4.0, 4.0)
    return final_result.astype(jnp.bfloat16)


def draw_segments(key, part):
    key = jax.random.fold_in(key, 9)
    groups = SEQUENCE_TOKENS // 8
    order = jax.random.permutation(key, groups - 1) + 1
    chosen = order[:DOCS - 1]
    flags = jnp.zeros((groups,), jnp.int32).at[chosen].set(1)
    numbers = jnp.cumsum(flags).astype(jnp.int32)
    return jnp.repeat(numbers, 8)


def steps_of(own_key, dims, cuts, smallest, high):
    def one(dim, parts):
        heights = jax.random.uniform(jax.random.fold_in(jax.random.fold_in(own_key, 6), dim), (parts,), jnp.float32, smallest / len(cuts), high / len(cuts))
        return jnp.repeat(jnp.exp(heights), dims[dim] // parts).reshape((-1,) + (1,) * (len(dims) - dim - 1))

    level = one(*cuts[0])
    for cut in cuts[1:]:
        level = level * one(*cut)
    return level


def scatter_about(key, dims, deviation, limit, cuts=(), kind=jnp.bfloat16):
    values = deviation * jax.random.normal(key, dims, jnp.float32)
    if cuts:
        values = values * steps_of(key, dims, cuts, -0.22, 0.18)
    return jnp.clip(values, -limit, limit).astype(kind)


def setup_inputs(seed: int = 0) -> dict:
    key_of = jax.random.split(jax.random.key(seed), 7)
    return {
        "queries": draw_queries(jax.random.fold_in(key_of[6], 71), 0),
        "keys": draw_keys(jax.random.fold_in(key_of[6], 71), 0),
        "values": scatter_about(key_of[2], (SEQUENCE_TOKENS, KEY_VALUE_HEADS * HEAD_SIZE), 1.0, 6.0, ((0, 8), (1, 4))),
        "grad_out": scatter_about(key_of[3], (SEQUENCE_TOKENS, D), 1.0, 6.0, ((0, 8), (1, 4))),
        "out_weight": scatter_about(key_of[4], (D, QUERY_HEADS * HEAD_SIZE), D ** -0.5, 0.09375, ((1, 4),)),
        "segments": draw_segments(jax.random.fold_in(key_of[6], 71), 0),
    }


def reference(queries, keys, values, grad_out, out_weight, segments):
    group_ratio = QUERY_HEADS // KEY_VALUE_HEADS
    scale = HEAD_SIZE ** -0.5
    upstream = jnp.dot(grad_out, out_weight, preferred_element_type=jnp.float32).astype(jnp.bfloat16)
    block = min(512, SEQUENCE_TOKENS)
    count = SEQUENCE_TOKENS // block
    positions = jnp.arange(SEQUENCE_TOKENS, dtype=jnp.int32)

    def single_group(group):
        col_q = (group * group_ratio * HEAD_SIZE).astype(jnp.int32)
        col_k = (group * HEAD_SIZE).astype(jnp.int32)
        query_all = lax.dynamic_slice_in_dim(queries, col_q, group_ratio * HEAD_SIZE, 1).reshape(SEQUENCE_TOKENS, group_ratio, HEAD_SIZE)
        upstream_all = lax.dynamic_slice_in_dim(upstream, col_q, group_ratio * HEAD_SIZE, 1).reshape(SEQUENCE_TOKENS, group_ratio, HEAD_SIZE)
        key_all = lax.dynamic_slice_in_dim(keys, col_k, HEAD_SIZE, 1).astype(jnp.float32)
        value_all = lax.dynamic_slice_in_dim(values, col_k, HEAD_SIZE, 1).astype(jnp.float32)

        def step(carry, index):
            key_acc, value_acc = carry
            start = (index * block).astype(jnp.int32)
            query_blk = lax.dynamic_slice_in_dim(query_all, start, block, 0).astype(jnp.float32)
            up_blk = lax.dynamic_slice_in_dim(upstream_all, start, block, 0).astype(jnp.float32)
            qpos = lax.dynamic_slice_in_dim(positions, start, block, 0)
            qseg = lax.dynamic_slice_in_dim(segments, start, block, 0)
            allowed = (positions[None, :] <= qpos[:, None]) & (segments[None, :] == qseg[:, None])
            scores = jnp.einsum("qrd,kd->rqk", query_blk, key_all) * scale
            scores = jnp.where(allowed[None], scores, jnp.float32(-1e30))
            top = jnp.max(scores, axis=-1, keepdims=True)
            lse = top + jnp.log(jnp.sum(jnp.where(allowed[None], jnp.exp(scores - top), 0.0), axis=-1, keepdims=True))
            probs = jnp.where(allowed[None], jnp.exp(scores - lse), 0.0)
            dprobs = jnp.einsum("qrd,kd->rqk", up_blk, value_all)
            delta = jnp.sum(probs * dprobs, axis=-1, keepdims=True)
            dscores = probs * (dprobs - delta)
            probs_low = probs.astype(jnp.bfloat16).astype(jnp.float32)
            dscores_low = dscores.astype(jnp.bfloat16).astype(jnp.float32)
            query_grad = (jnp.einsum("rqk,kd->qrd", dscores_low, key_all) * scale).astype(jnp.bfloat16)
            key_acc = key_acc + jnp.einsum("rqk,qrd->kd", dscores_low, query_blk)
            value_acc = value_acc + jnp.einsum("rqk,qrd->kd", probs_low, up_blk)
            return (key_acc, value_acc), query_grad

        zeros = jnp.zeros((SEQUENCE_TOKENS, HEAD_SIZE), jnp.float32)
        (key_acc, value_acc), query_parts = lax.scan(step, (zeros, zeros), jnp.arange(count, dtype=jnp.int32))
        query_grad = query_parts.reshape(SEQUENCE_TOKENS, group_ratio, HEAD_SIZE)
        return query_grad, (key_acc * scale).astype(jnp.bfloat16), value_acc.astype(jnp.bfloat16)

    query_grad_local, key_grad_local, value_grad_local = lax.map(single_group, jnp.arange(KEY_VALUE_HEADS, dtype=jnp.int32))
    query_grad = jnp.transpose(query_grad_local, (1, 0, 2, 3)).reshape(SEQUENCE_TOKENS, QUERY_HEADS * HEAD_SIZE)
    key_gradient = jnp.transpose(key_grad_local, (1, 0, 2)).reshape(SEQUENCE_TOKENS, KEY_VALUE_HEADS * HEAD_SIZE)
    value_gradient = jnp.transpose(value_grad_local, (1, 0, 2)).reshape(SEQUENCE_TOKENS, KEY_VALUE_HEADS * HEAD_SIZE)
    return query_grad, key_gradient, value_gradient
```

```python
import functools

import jax
import jax.numpy as jnp
from jax import lax
from jax.experimental import pallas as pl
from jax.experimental.pallas import tpu as pltpu
from jax.sharding import PartitionSpec as P

QUERY_HEADS = 32
KEY_VALUE_HEADS = 8
HEAD_SIZE = 128
RATIO = QUERY_HEADS // KEY_VALUE_HEADS
SEG_ROWS = 16
LOG2E = 1.4426950408889634
MESH = pl.DeviceIdType.MESH
F32 = jnp.float32
BF16 = jnp.bfloat16


def dot(a, b, ca, cb):
    return lax.dot_general(a, b, (((ca,), (cb,)), ((), ())), preferred_element_type=F32)


def kernel(
    stages, q_in, k_in, v_in, g_in, w_hbm, seg_in,
    q_out, k_out, v_out,
    wbuf, gbuf, acc, kv, ky, qbuf, ubuf, usend, mst, lst, wst, ones,
    dq, dqs, dqr, own, rs, ret, fins, finr,
    w_sem, gx_s, gx_r, gc_s, gc_r, gf_s, gf_r, kv_s, kv_r, ret_s, ret_r,
    misc_s, misc_r, fin_s, fin_r,
):
    rows = k_in.shape[0]
    pair = 2 * rows
    hs = HEAD_SIZE
    gw = RATIO * hs
    half = g_in.shape[1] // 2
    scale = HEAD_SIZE ** -0.5
    ctx = lax.axis_index("ctx")
    tp = lax.axis_index("tp")
    s, y = ctx // 2, ctx % 2
    z = 1 - y
    x, c = tp // 2, tp % 2
    sib = (2 * s + z, tp)
    down = (2 * lax.rem(s + 1, stages) + y, tp)
    up = (2 * lax.rem(s + stages - 1, stages) + y, tp)
    xnb = (ctx, 2 * (1 - x) + c)
    core = (ctx, 2 * x + 1 - c)
    t_own, t_core, t_x, t_f = tp, 2 * x + 1 - c, 2 * (1 - x) + c, 2 * (1 - x) + 1 - c

    def remote(src, dst, a, b, dev):
        return pltpu.make_async_remote_copy(
            src_ref=src, dst_ref=dst, send_sem=a, recv_sem=b, device_id=dev, device_id_type=MESH
        )

    def w_copy(t, h):
        i = 2 * t + h
        return pltpu.make_async_copy(w_hbm.at[pl.ds(i * half, half)], wbuf.at[i], w_sem.at[i])

    for t in (t_own, t_core, t_x, t_f):
        for h in range(2):
            w_copy(t, h).start()

    def fill(dst, g):
        cols = pl.ds(pl.multiple_of(g * hs, hs), hs)
        dst[0:rows, :] = k_in[:, cols]
        dst[rows : 2 * rows, :] = v_in[:, cols]
        dst[2 * rows :, :] = jnp.broadcast_to(seg_in[...].astype(F32), (SEG_ROWS, rows)).astype(BF16)

    fill(kv.at[s, y], y)
    fill(ky, z)

    barrier = pltpu.get_barrier_semaphore()
    for dev in (sib, down, up, xnb, core):
        pl.semaphore_signal(barrier, inc=1, device_id=dev, device_id_type=MESH)
    pl.semaphore_wait(barrier, 5)

    def chain(k, p):
        return remote(kv.at[k, p], kv.at[k, p], kv_s.at[k, p], kv_r.at[k, p], down)

    ky_copy = remote(ky, kv.at[s, y], misc_s.at[0], misc_r.at[0], sib)
    q_copy = remote(
        q_in.at[:, pl.ds(pl.multiple_of(z * gw, gw), gw)], qbuf.at[y], misc_s.at[1], misc_r.at[1], sib
    )
    u_copy = remote(usend, ubuf.at[y], misc_s.at[2], misc_r.at[2], sib)
    dq_copy = remote(dqs, dqr, misc_s.at[3], misc_r.at[3], sib)
    gx = [
        remote(g_in.at[:, h * half : (h + 1) * half], gbuf.at[t_own, h], gx_s.at[h], gx_r.at[h], xnb)
        for h in range(2)
    ]
    gc = [
        remote(g_in.at[:, h * half : (h + 1) * half], gbuf.at[t_own, h], gc_s.at[h], gc_r.at[h], core)
        for h in range(2)
    ]
    gf = [remote(gbuf.at[t_x, h], gbuf.at[t_x, h], gf_s.at[h], gf_r.at[h], core) for h in range(2)]
    last = s == stages - 1

    ky_copy.start()
    gx[0].start()

    @pl.when(jnp.logical_not(last))
    def _():
        chain(s, y).start()

    gx[1].start()
    gc[0].start()
    gc[1].start()
    q_copy.start()

    qbuf[y] = q_in[:, pl.ds(pl.multiple_of(y * gw, gw), gw)]

    def product(left, t, h):
        w_copy(t, h).wait()
        return dot(left, wbuf[2 * t + h], 1, 0)

    acc[...] = product(g_in[:, 0:half], t_own, 0)
    acc[...] += product(g_in[:, half:], t_own, 1)

    ky_copy.wait_recv()

    @pl.when(jnp.logical_not(last))
    def _():
        chain(s, z).start()

    for h in range(2):
        gc[h].wait_recv()
        acc[...] += product(gbuf[t_core, h], t_core, h)
    gx[0].wait_recv()
    gf[0].start()
    acc[...] += product(gbuf[t_x, 0], t_x, 0)

    def arrive(k):
        for p in range(2):
            chain(k, p).wait_recv()

            @pl.when(jnp.logical_not(last))
            def _():
                chain(k, p).start()

    @pl.when(s >= 1)
    def _():
        arrive(s - 1)

    gx[1].wait_recv()
    gf[1].start()
    acc[...] += product(gbuf[t_x, 1], t_x, 1)
    for h in range(2):
        gf[h].wait_recv()
        acc[...] += product(gbuf[t_f, h], t_f, h)
    usend[...] = acc[:, pl.ds(pl.multiple_of(z * gw, gw), gw)].astype(BF16)
    u_copy.start()
    ubuf[y] = acc[:, pl.ds(pl.multiple_of(y * gw, gw), gw)].astype(BF16)

    @pl.when(jnp.logical_not(last))
    def _():
        def body(i, carry):
            arrive(s - 2 - i)
            return carry

        lax.fori_loop(0, s - 1, body, 0)

    q_copy.wait_recv()
    u_copy.wait_recv()

    mst[...] = jnp.full(mst.shape, -1e20, F32)
    lst[...] = jnp.zeros(lst.shape, F32)
    wst[...] = jnp.zeros(wst.shape, F32)
    ones[...] = jnp.zeros(ones.shape, F32)
    dq[...] = jnp.zeros(dq.shape, F32)

    def heads(ref, r):
        return ref[:, :, r * hs : (r + 1) * hs].reshape(pair, hs)

    def block(k):
        keys = kv[k, :, 0:rows, :].reshape(pair, hs)
        values = kv[k, :, rows : 2 * rows, :].reshape(pair, hs)
        begin = (s + 1) * pair - ones[0:1, :].astype(jnp.int32)
        qpos = s * pair + lax.broadcasted_iota(jnp.int32, (1, pair), 1)
        low = jnp.where(qpos < begin, 0, begin)
        kpos = k * pair + lax.broadcasted_iota(jnp.int32, (pair, pair), 0)
        return keys, values, (kpos <= qpos) & (kpos >= low)

    def scores(keys, values, allowed, r):
        sc = dot(keys, heads(qbuf, r), 1, 1) * (scale * LOG2E)
        return jnp.where(allowed, sc, -1e30), dot(values, heads(ubuf, r), 1, 1)

    def statistics(i, carry):
        k = s - i

        @pl.when(last & (k < s - 1))
        def _():
            for p in range(2):
                chain(k, p).wait_recv()

        seg = kv[k, :, 2 * rows :, :].astype(F32).reshape(2 * SEG_ROWS, rows)
        count = jnp.sum(jnp.sum(seg, axis=0, keepdims=True), axis=1, keepdims=True) * (1.0 / SEG_ROWS)
        ones[...] += jnp.broadcast_to(count, ones.shape)
        keys, values, allowed = block(k)
        for r in range(RATIO):
            sc, dp = scores(keys, values, allowed, r)
            old = mst[r : r + 1, :]
            new = jnp.maximum(old, jnp.max(sc, axis=0, keepdims=True))
            pr = jnp.exp2(sc - new)
            factor = jnp.exp2(old - new)
            mst[r : r + 1, :] = new
            lst[r : r + 1, :] = lst[r : r + 1, :] * factor + jnp.sum(pr, axis=0, keepdims=True)
            wst[r : r + 1, :] = wst[r : r + 1, :] * factor + jnp.sum(pr * dp, axis=0, keepdims=True)
        return carry

    lax.fori_loop(0, s + 1, statistics, 0)
    mst[...] = mst[...] + jnp.log2(lst[...])
    wst[...] = wst[...] / lst[...]

    def back(k, p):
        return remote(rs.at[k, p], ret.at[k, p], ret_s.at[k, p], ret_r.at[k, p], up)

    def gradients(k, carry):
        keys, values, allowed = block(k)
        dk = jnp.zeros((pair, hs), F32)
        dv = jnp.zeros((pair, hs), F32)
        for r in range(RATIO):
            sc, dp = scores(keys, values, allowed, r)
            pr = jnp.exp2(sc - mst[r : r + 1, :])
            ds = (pr * (dp - wst[r : r + 1, :])).astype(BF16)
            dv += dot(pr.astype(BF16), heads(ubuf, r), 1, 0)
            dk += dot(ds, heads(qbuf, r), 1, 0)
            dq[r] += dot(ds, keys, 0, 0)
        own[k, 0] = dk * scale
        own[k, 1] = dv

        @pl.when(last & (k < s))
        def _():
            for p in range(2):
                rs[k, p] = own[k, p].astype(BF16)
                back(k, p).start()

        return carry

    lax.fori_loop(0, s + 1, gradients, 0)

    for r in range(RATIO):
        dqs[:, r * hs : (r + 1) * hs] = (
            dq[r, pl.ds(pl.multiple_of(z * rows, rows), rows), :] * scale
        ).astype(BF16)
    dq_copy.start()
    for r in range(RATIO):
        q_out[:, pl.ds(pl.multiple_of(y * gw, gw) + r * hs, hs)] = (
            dq[r, pl.ds(pl.multiple_of(y * rows, rows), rows), :] * scale
        ).astype(BF16)

    @pl.when(jnp.logical_not(last))
    def _():
        def body(k, carry):
            for p in range(2):
                back(k, p).wait_recv()
                rs[k, p] = (own[k, p] + ret[k, p].astype(F32)).astype(BF16)
                back(k, p).start()
            return carry

        lax.fori_loop(0, s, body, 0)
        for p in range(2):
            back(s, p).wait_recv()
            own[s, p] = own[s, p] + ret[s, p].astype(F32)

    fin = [remote(fins.at[p], finr.at[p], fin_s.at[p], fin_r.at[p], sib) for p in range(2)]
    for p in range(2):
        fins[p] = own[s, p, pl.ds(pl.multiple_of(z * rows, rows), rows), :].astype(BF16)
        fin[p].start()
    mine = pl.ds(pl.multiple_of(y * hs, hs), hs)
    theirs = pl.ds(pl.multiple_of(z * hs, hs), hs)
    for p, out in enumerate((k_out, v_out)):
        out[:, mine] = own[s, p, pl.ds(pl.multiple_of(y * rows, rows), rows), :].astype(BF16)
    dq_copy.wait_recv()
    q_out[:, pl.ds(pl.multiple_of(z * gw, gw), gw)] = dqr[...]
    for p, out in enumerate((k_out, v_out)):
        fin[p].wait_recv()
        out[:, theirs] = finr[p]

    for copy in (ky_copy, q_copy, u_copy, dq_copy, *gx, *gc, *gf, *fin):
        copy.wait_send()

    @pl.when(jnp.logical_not(last))
    def _():
        def body(k, carry):
            for p in range(2):
                chain(k, p).wait_send()
            return carry

        lax.fori_loop(0, s + 1, body, 0)

    def drain(k, carry):
        for p in range(2):
            back(k, p).wait_send()
        return carry

    lax.fori_loop(0, s, drain, 0)


def per_device(stages, queries, keys, values, grad_out, out_weight, segments):
    rows, wide = queries.shape
    depth = grad_out.shape[1]
    pair, hs, gw = 2 * rows, HEAD_SIZE, RATIO * HEAD_SIZE
    vmem = pl.BlockSpec(memory_space=pltpu.VMEM)
    dma = pltpu.SemaphoreType.DMA
    return pl.pallas_call(
        functools.partial(kernel, stages),
        out_shape=(
            jax.ShapeDtypeStruct(queries.shape, BF16),
            jax.ShapeDtypeStruct(keys.shape, BF16),
            jax.ShapeDtypeStruct(values.shape, BF16),
        ),
        in_specs=[vmem, vmem, vmem, vmem, pl.BlockSpec(memory_space=pl.ANY), vmem],
        out_specs=(vmem, vmem, vmem),
        scratch_shapes=[
            pltpu.VMEM((8, depth // 2, wide), BF16),
            pltpu.VMEM((4, 2, rows, depth // 2), BF16),
            pltpu.VMEM((rows, wide), F32),
            pltpu.VMEM((stages, 2, pair + SEG_ROWS, hs), BF16),
            pltpu.VMEM((pair + SEG_ROWS, hs), BF16),
            pltpu.VMEM((2, rows, gw), BF16),
            pltpu.VMEM((2, rows, gw), BF16),
            pltpu.VMEM((rows, gw), BF16),
            pltpu.VMEM((RATIO, pair), F32),
            pltpu.VMEM((RATIO, pair), F32),
            pltpu.VMEM((RATIO, pair), F32),
            pltpu.VMEM((8, pair), F32),
            pltpu.VMEM((RATIO, pair, hs), F32),
            pltpu.VMEM((rows, gw), BF16),
            pltpu.VMEM((rows, gw), BF16),
            pltpu.VMEM((stages, 2, pair, hs), F32),
            pltpu.VMEM((stages, 2, pair, hs), BF16),
            pltpu.VMEM((stages, 2, pair, hs), BF16),
            pltpu.VMEM((2, rows, hs), BF16),
            pltpu.VMEM((2, rows, hs), BF16),
            dma((8,)),
            dma((2,)), dma((2,)), dma((2,)), dma((2,)), dma((2,)), dma((2,)),
            dma((stages, 2)), dma((stages, 2)), dma((stages, 2)), dma((stages, 2)),
            dma((4,)), dma((4,)), dma((2,)), dma((2,)),
        ],
        compiler_params=pltpu.CompilerParams(
            collective_id=0, has_side_effects=True, vmem_limit_bytes=56 * 1024 * 1024
        ),
        name="attention_backward",
    )(queries, keys, values, grad_out, out_weight, segments.reshape(1, rows))


def solution(mesh):
    in_specs = (
        P("ctx", "tp"),
        P("ctx", "tp"),
        P("ctx", "tp"),
        P("ctx", "tp"),
        P(None, "tp"),
        P("ctx"),
    )
    out_specs = (P("ctx", "tp"), P("ctx", "tp"), P("ctx", "tp"))
    return jax.shard_map(
        functools.partial(per_device, mesh.shape["ctx"] // 2),
        mesh=mesh, in_specs=in_specs, out_specs=out_specs, check_vma=False,
    )
```

```python
import functools

import jax
import jax.numpy as jnp
from jax import lax
from jax.experimental import pallas as pl
from jax.experimental.pallas import tpu as pltpu
from jax.sharding import PartitionSpec as P

QUERY_HEADS = 32
KEY_VALUE_HEADS = 8
HEAD_SIZE = 128
RATIO = QUERY_HEADS // KEY_VALUE_HEADS
SEG_ROWS = 16
KEPT_STAGES = 8
LOG2E = 1.4426950408889634
MESH = pl.DeviceIdType.MESH
F32 = jnp.float32
BF16 = jnp.bfloat16


def dot(a, b, ca, cb):
    return lax.dot_general(a, b, (((ca,), (cb,)), ((), ())), preferred_element_type=F32)


def kernel(
    stages, q_in, k_in, v_in, g_in, w_hbm, seg_in,
    q_out, k_out, v_out,
    wbuf, gbuf, acc, kv, ky, qbuf, ubuf, usend, mst, lst, wst, ones, ot, kept,
    dq, dqs, dqr, own, rs, ret, fins, finr,
    w_sem, gx_s, gx_r, gc_s, gc_r, gf_s, gf_r, kv_s, kv_r, ret_s, ret_r,
    misc_s, misc_r, fin_s, fin_r,
):
    rows = k_in.shape[0]
    pair = 2 * rows
    hs = HEAD_SIZE
    gw = RATIO * hs
    keep = stages <= KEPT_STAGES
    half = g_in.shape[1] // 2
    scale = HEAD_SIZE ** -0.5
    ctx = lax.axis_index("ctx")
    tp = lax.axis_index("tp")
    s, y = ctx // 2, ctx % 2
    z = 1 - y
    x, c = tp // 2, tp % 2
    sib = (2 * s + z, tp)
    down = (2 * lax.rem(s + 1, stages) + y, tp)
    up = (2 * lax.rem(s + stages - 1, stages) + y, tp)
    xnb = (ctx, 2 * (1 - x) + c)
    core = (ctx, 2 * x + 1 - c)
    t_own, t_core, t_x, t_f = tp, 2 * x + 1 - c, 2 * (1 - x) + c, 2 * (1 - x) + 1 - c

    barrier = pltpu.get_barrier_semaphore()
    for dev in (sib, down, up, xnb, core):
        pl.semaphore_signal(barrier, inc=1, device_id=dev, device_id_type=MESH)

    def remote(src, dst, a, b, dev):
        return pltpu.make_async_remote_copy(
            src_ref=src, dst_ref=dst, send_sem=a, recv_sem=b, device_id=dev, device_id_type=MESH
        )

    def w_copy(t, h):
        i = 2 * t + h
        return pltpu.make_async_copy(w_hbm.at[pl.ds(i * half, half)], wbuf.at[i], w_sem.at[i])

    for t in (t_own, t_core, t_x, t_f):
        for h in range(2):
            w_copy(t, h).start()

    def fill(dst, g):
        cols = pl.ds(pl.multiple_of(g * hs, hs), hs)
        dst[0:rows, :] = k_in[:, cols]
        dst[rows : 2 * rows, :] = v_in[:, cols]
        dst[2 * rows :, :] = jnp.broadcast_to(seg_in[...].astype(F32), (SEG_ROWS, rows)).astype(BF16)

    fill(kv.at[s, y], y)
    fill(ky, z)

    pl.semaphore_wait(barrier, 5)

    def chain(k, p):
        return remote(kv.at[k, p], kv.at[k, p], kv_s.at[k, p], kv_r.at[k, p], down)

    ky_copy = remote(ky, kv.at[s, y], misc_s.at[0], misc_r.at[0], sib)
    q_copy = remote(
        q_in.at[:, pl.ds(pl.multiple_of(z * gw, gw), gw)], qbuf.at[y], misc_s.at[1], misc_r.at[1], sib
    )
    u_copy = remote(usend, ubuf.at[y], misc_s.at[2], misc_r.at[2], sib)
    dq_copy = remote(dqs, dqr, misc_s.at[3], misc_r.at[3], sib)
    gx = [
        remote(g_in.at[:, h * half : (h + 1) * half], gbuf.at[t_own, h], gx_s.at[h], gx_r.at[h], xnb)
        for h in range(2)
    ]
    gc = [
        remote(g_in.at[:, h * half : (h + 1) * half], gbuf.at[t_own, h], gc_s.at[h], gc_r.at[h], core)
        for h in range(2)
    ]
    gf = [remote(gbuf.at[t_x, h], gbuf.at[t_x, h], gf_s.at[h], gf_r.at[h], core) for h in range(2)]
    last = s == stages - 1

    ky_copy.start()
    gx[0].start()

    @pl.when(jnp.logical_not(last))
    def _():
        chain(s, y).start()

    gx[1].start()
    gc[0].start()
    gc[1].start()
    q_copy.start()

    qbuf[y] = q_in[:, pl.ds(pl.multiple_of(y * gw, gw), gw)]

    def product(left, t, h):
        w_copy(t, h).wait()
        return dot(left, wbuf[2 * t + h], 1, 0)

    acc[...] = product(g_in[:, 0:half], t_own, 0)
    acc[...] += product(g_in[:, half:], t_own, 1)

    ky_copy.wait_recv()

    @pl.when(jnp.logical_not(last))
    def _():
        chain(s, z).start()

    for h in range(2):
        gc[h].wait_recv()
        acc[...] += product(gbuf[t_core, h], t_core, h)
    gx[0].wait_recv()
    gf[0].start()

    def arrive(k):
        for p in range(2):
            chain(k, p).wait_recv()

            @pl.when(jnp.logical_not(last))
            def _():
                chain(k, p).start()

    @pl.when(s >= 1)
    def _():
        arrive(s - 1)

    acc[...] += product(gbuf[t_x, 0], t_x, 0)
    gx[1].wait_recv()
    gf[1].start()

    @pl.when((s >= 2) & jnp.logical_not(last))
    def _():
        arrive(s - 2)

    acc[...] += product(gbuf[t_x, 1], t_x, 1)
    for h in range(2):
        gf[h].wait_recv()
        acc[...] += product(gbuf[t_f, h], t_f, h)
    usend[...] = acc[:, pl.ds(pl.multiple_of(z * gw, gw), gw)].astype(BF16)
    u_copy.start()
    ubuf[y] = acc[:, pl.ds(pl.multiple_of(y * gw, gw), gw)].astype(BF16)

    @pl.when(jnp.logical_not(last))
    def _():
        def body(i, carry):
            arrive(s - 3 - i)
            return carry

        lax.fori_loop(0, s - 2, body, 0)

    q_copy.wait_recv()

    mst[...] = jnp.full(mst.shape, -1e20, F32)
    lst[...] = jnp.zeros(lst.shape, F32)
    ot[...] = jnp.zeros(ot.shape, F32)
    ones[...] = jnp.zeros(ones.shape, F32)
    dq[...] = jnp.zeros(dq.shape, F32)

    def heads(ref, r):
        return ref[:, :, r * hs : (r + 1) * hs].reshape(pair, hs)

    def pieces(k):
        return kv[k, :, 0:rows, :].reshape(pair, hs), kv[k, :, rows : 2 * rows, :].reshape(pair, hs)

    def block(k):
        keys, values = pieces(k)
        begin = (s + 1) * pair - ones[0:1, :].astype(jnp.int32)
        qpos = s * pair + lax.broadcasted_iota(jnp.int32, (1, pair), 1)
        low = jnp.where(qpos < begin, 0, begin)
        kpos = k * pair + lax.broadcasted_iota(jnp.int32, (pair, pair), 0)
        return keys, values, (kpos <= qpos) & (kpos >= low)

    def scores(keys, allowed, r):
        sc = dot(keys, heads(qbuf, r), 1, 1) * (scale * LOG2E)
        return jnp.where(allowed, sc, -1e30)

    def statistics(i, carry):
        k = s - i

        @pl.when(last & (k < s - 1))
        def _():
            for p in range(2):
                chain(k, p).wait_recv()

        seg = kv[k, :, 2 * rows :, :].astype(F32).reshape(2 * SEG_ROWS, rows)
        count = jnp.sum(jnp.sum(seg, axis=0, keepdims=True), axis=1, keepdims=True) * (1.0 / SEG_ROWS)
        ones[...] += jnp.broadcast_to(count, ones.shape)
        keys, values, allowed = block(k)
        turned = values.T
        for r in range(RATIO):
            sc = scores(keys, allowed, r)
            if keep:
                kept[k, r] = sc
            old = mst[r : r + 1, :]
            new = jnp.maximum(old, jnp.max(sc, axis=0, keepdims=True))
            pr = jnp.exp2(sc - new)
            factor = jnp.exp2(old - new)
            mst[r : r + 1, :] = new
            lst[r : r + 1, :] = lst[r : r + 1, :] * factor + jnp.sum(pr, axis=0, keepdims=True)
            ot[r] = ot[r] * factor + dot(turned, pr.astype(BF16), 1, 0)
        return carry

    lax.fori_loop(0, s + 1, statistics, 0)
    u_copy.wait_recv()
    for r in range(RATIO):
        wst[r : r + 1, :] = jnp.sum(heads(ubuf, r).astype(F32).T * ot[r], axis=0, keepdims=True)
    mst[...] = mst[...] + jnp.log2(lst[...])
    wst[...] = wst[...] / lst[...]

    def back(k, p):
        return remote(rs.at[k, p], ret.at[k, p], ret_s.at[k, p], ret_r.at[k, p], up)

    def gradients(k, carry):
        if keep:
            keys, values = pieces(k)
        else:
            keys, values, allowed = block(k)
        turned = keys.T
        dk = jnp.zeros((pair, hs), F32)
        dv = jnp.zeros((pair, hs), F32)
        for r in range(RATIO):
            sc = kept[k, r] if keep else scores(keys, allowed, r)
            dp = dot(values, heads(ubuf, r), 1, 1)
            pr = jnp.exp2(sc - mst[r : r + 1, :])
            ds = (pr * (dp - wst[r : r + 1, :])).astype(BF16)
            dv += dot(pr.astype(BF16), heads(ubuf, r), 1, 0)
            dk += dot(ds, heads(qbuf, r), 1, 0)
            dq[r] += dot(turned, ds, 1, 0)
        own[k, 0] = dk * scale
        own[k, 1] = dv

        @pl.when(last & (k < s))
        def _():
            for p in range(2):
                rs[k, p] = own[k, p].astype(BF16)
                back(k, p).start()

        return carry

    lax.fori_loop(0, s + 1, gradients, 0)

    for r in range(RATIO):
        dqs[:, r * hs : (r + 1) * hs] = (
            dq[r, :, pl.ds(pl.multiple_of(z * rows, rows), rows)] * scale
        ).T.astype(BF16)
    dq_copy.start()
    for r in range(RATIO):
        q_out[:, pl.ds(pl.multiple_of(y * gw, gw) + r * hs, hs)] = (
            dq[r, :, pl.ds(pl.multiple_of(y * rows, rows), rows)] * scale
        ).T.astype(BF16)

    @pl.when(jnp.logical_not(last))
    def _():
        def body(k, carry):
            for p in range(2):
                back(k, p).wait_recv()
                rs[k, p] = (own[k, p] + ret[k, p].astype(F32)).astype(BF16)
                back(k, p).start()
            return carry

        lax.fori_loop(0, s, body, 0)
        for p in range(2):
            back(s, p).wait_recv()
            own[s, p] = own[s, p] + ret[s, p].astype(F32)

    fin = [remote(fins.at[p], finr.at[p], fin_s.at[p], fin_r.at[p], sib) for p in range(2)]
    for p in range(2):
        fins[p] = own[s, p, pl.ds(pl.multiple_of(z * rows, rows), rows), :].astype(BF16)
        fin[p].start()
    mine = pl.ds(pl.multiple_of(y * hs, hs), hs)
    theirs = pl.ds(pl.multiple_of(z * hs, hs), hs)
    for p, out in enumerate((k_out, v_out)):
        out[:, mine] = own[s, p, pl.ds(pl.multiple_of(y * rows, rows), rows), :].astype(BF16)
    dq_copy.wait_recv()
    q_out[:, pl.ds(pl.multiple_of(z * gw, gw), gw)] = dqr[...]
    for p, out in enumerate((k_out, v_out)):
        fin[p].wait_recv()
        out[:, theirs] = finr[p]

    for copy in (ky_copy, q_copy, u_copy, dq_copy, *gx, *gc, *gf, *fin):
        copy.wait_send()

    @pl.when(jnp.logical_not(last))
    def _():
        def body(k, carry):
            for p in range(2):
                chain(k, p).wait_send()
            return carry

        lax.fori_loop(0, s + 1, body, 0)

    def drain(k, carry):
        for p in range(2):
            back(k, p).wait_send()
        return carry

    lax.fori_loop(0, s, drain, 0)


def hand_over(a, b, c, x, y, z, sem):
    copies = [pltpu.make_async_copy(p, q, sem.at[i]) for i, (p, q) in enumerate(((a, x), (b, y), (c, z)))]
    for copy in copies:
        copy.start()
    for copy in copies:
        copy.wait()


def per_device(stages, queries, keys, values, grad_out, out_weight, segments):
    rows, wide = queries.shape
    depth = grad_out.shape[1]
    pair, hs, gw = 2 * rows, HEAD_SIZE, RATIO * HEAD_SIZE
    vmem = pl.BlockSpec(memory_space=pltpu.VMEM)
    dma = pltpu.SemaphoreType.DMA
    grads = pl.pallas_call(
        functools.partial(kernel, stages),
        out_shape=(
            jax.ShapeDtypeStruct(queries.shape, BF16),
            jax.ShapeDtypeStruct(keys.shape, BF16),
            jax.ShapeDtypeStruct(values.shape, BF16),
        ),
        in_specs=[vmem, vmem, vmem, vmem, pl.BlockSpec(memory_space=pl.ANY), vmem],
        out_specs=(vmem, vmem, vmem),
        scratch_shapes=[
            pltpu.VMEM((8, depth // 2, wide), BF16),
            pltpu.VMEM((4, 2, rows, depth // 2), BF16),
            pltpu.VMEM((rows, wide), F32),
            pltpu.VMEM((stages, 2, pair + SEG_ROWS, hs), BF16),
            pltpu.VMEM((pair + SEG_ROWS, hs), BF16),
            pltpu.VMEM((2, rows, gw), BF16),
            pltpu.VMEM((2, rows, gw), BF16),
            pltpu.VMEM((rows, gw), BF16),
            pltpu.VMEM((RATIO, pair), F32),
            pltpu.VMEM((RATIO, pair), F32),
            pltpu.VMEM((RATIO, pair), F32),
            pltpu.VMEM((8, pair), F32),
            pltpu.VMEM((RATIO, hs, pair), F32),
            pltpu.VMEM((stages if stages <= KEPT_STAGES else 1, RATIO, pair, pair), F32),
            pltpu.VMEM((RATIO, hs, pair), F32),
            pltpu.VMEM((rows, gw), BF16),
            pltpu.VMEM((rows, gw), BF16),
            pltpu.VMEM((stages, 2, pair, hs), F32),
            pltpu.VMEM((stages, 2, pair, hs), BF16),
            pltpu.VMEM((stages, 2, pair, hs), BF16),
            pltpu.VMEM((2, rows, hs), BF16),
            pltpu.VMEM((2, rows, hs), BF16),
            dma((8,)),
            dma((2,)), dma((2,)), dma((2,)), dma((2,)), dma((2,)), dma((2,)),
            dma((stages, 2)), dma((stages, 2)), dma((stages, 2)), dma((stages, 2)),
            dma((4,)), dma((4,)), dma((2,)), dma((2,)),
        ],
        compiler_params=pltpu.CompilerParams(
            collective_id=0, has_side_effects=True, vmem_limit_bytes=56 * 1024 * 1024
        ),
        name="attention_backward",
    )(queries, keys, values, grad_out, out_weight, segments.reshape(1, rows))
    anywhere = pl.BlockSpec(memory_space=pl.ANY)
    return pl.pallas_call(
        hand_over,
        out_shape=tuple(jax.ShapeDtypeStruct(a.shape, a.dtype) for a in grads),
        in_specs=[anywhere] * 3,
        out_specs=(anywhere,) * 3,
        scratch_shapes=[dma((3,))],
        compiler_params=pltpu.CompilerParams(vmem_limit_bytes=56 * 1024 * 1024),
        name="hand_over",
    )(*grads)


def solution(mesh):
    in_specs = (
        P("ctx", "tp"),
        P("ctx", "tp"),
        P("ctx", "tp"),
        P("ctx", "tp"),
        P(None, "tp"),
        P("ctx"),
    )
    out_specs = (P("ctx", "tp"), P("ctx", "tp"), P("ctx", "tp"))
    return jax.shard_map(
        functools.partial(per_device, mesh.shape["ctx"] // 2),
        mesh=mesh, in_specs=in_specs, out_specs=out_specs, check_vma=False,
    )
```

```python
import functools

import jax
import jax.numpy as jnp
from jax import lax
from jax.experimental import pallas as pl
from jax.experimental.pallas import tpu as pltpu
from jax.sharding import PartitionSpec as P

QUERY_HEADS = 32
KEY_VALUE_HEADS = 8
HEAD_SIZE = 128
RATIO = QUERY_HEADS // KEY_VALUE_HEADS
SEG_ROWS = 16
KEPT_STAGES = 8
LOG2E = 1.4426950408889634
MESH = pl.DeviceIdType.MESH
F32 = jnp.float32
BF16 = jnp.bfloat16


def dot(a, b, ca, cb):
    return lax.dot_general(a, b, (((ca,), (cb,)), ((), ())), preferred_element_type=F32)


def kernel(
    stages, q_in, k_in, v_in, g_in, w_hbm, seg_in,
    q_out, k_out, v_out,
    wbuf, gbuf, acc, kv, ky, qbuf, ubuf, usend, mst, lst, wst, ones, ot, kept,
    dq, dqs, dqr, own, rs, ret, retd, fins, finr,
    w_sem, gx_s, gx_r, gc_s, gc_r, gf_s, gf_r, kv_s, kv_r, ret_s, ret_r, dia_s, dia_r,
    misc_s, misc_r, fin_s, fin_r,
):
    rows = k_in.shape[0]
    pair = 2 * rows
    hs = HEAD_SIZE
    gw = RATIO * hs
    keep = stages <= KEPT_STAGES
    half = g_in.shape[1] // 2
    scale = HEAD_SIZE ** -0.5
    ctx = lax.axis_index("ctx")
    tp = lax.axis_index("tp")
    s, y = ctx // 2, ctx % 2
    z = 1 - y
    x, c = tp // 2, tp % 2
    sib = (2 * s + z, tp)
    down = (2 * lax.rem(s + 1, stages) + y, tp)
    up = (2 * lax.rem(s + stages - 1, stages) + y, tp)
    down_d = (2 * lax.rem(s + 1, stages) + z, tp)
    up_d = (2 * lax.rem(s + stages - 1, stages) + z, tp)
    xnb = (ctx, 2 * (1 - x) + c)
    core = (ctx, 2 * x + 1 - c)
    t_own, t_core, t_x, t_f = tp, 2 * x + 1 - c, 2 * (1 - x) + c, 2 * (1 - x) + 1 - c

    barrier = pltpu.get_barrier_semaphore()
    for dev in (sib, down, up, down_d, up_d, xnb, core):
        pl.semaphore_signal(barrier, inc=1, device_id=dev, device_id_type=MESH)

    def remote(src, dst, a, b, dev):
        return pltpu.make_async_remote_copy(
            src_ref=src, dst_ref=dst, send_sem=a, recv_sem=b, device_id=dev, device_id_type=MESH
        )

    def w_copy(t, h):
        i = 2 * t + h
        return pltpu.make_async_copy(w_hbm.at[pl.ds(i * half, half)], wbuf.at[i], w_sem.at[i])

    for t in (t_own, t_core, t_x, t_f):
        for h in range(2):
            w_copy(t, h).start()

    def fill(dst, g):
        cols = pl.ds(pl.multiple_of(g * hs, hs), hs)
        dst[0:rows, :] = k_in[:, cols]
        dst[rows : 2 * rows, :] = v_in[:, cols]
        dst[2 * rows :, :] = jnp.broadcast_to(seg_in[...].astype(F32), (SEG_ROWS, rows)).astype(BF16)

    fill(kv.at[s, y], y)
    fill(ky, z)

    pl.semaphore_wait(barrier, 7)

    def chain(k, p):
        return remote(kv.at[k, p], kv.at[k, p], kv_s.at[k, p], kv_r.at[k, p], down)

    ky_copy = remote(ky, kv.at[s, y], misc_s.at[0], misc_r.at[0], sib)
    q_copy = remote(
        q_in.at[:, pl.ds(pl.multiple_of(z * gw, gw), gw)], qbuf.at[y], misc_s.at[1], misc_r.at[1], sib
    )
    u_copy = remote(usend, ubuf.at[y], misc_s.at[2], misc_r.at[2], sib)
    dq_copy = remote(dqs, dqr, misc_s.at[3], misc_r.at[3], sib)
    gx = [
        remote(g_in.at[:, h * half : (h + 1) * half], gbuf.at[t_own, h], gx_s.at[h], gx_r.at[h], xnb)
        for h in range(2)
    ]
    gc = [
        remote(g_in.at[:, h * half : (h + 1) * half], gbuf.at[t_own, h], gc_s.at[h], gc_r.at[h], core)
        for h in range(2)
    ]
    gf = [remote(gbuf.at[t_x, h], gbuf.at[t_x, h], gf_s.at[h], gf_r.at[h], core) for h in range(2)]
    last = s == stages - 1

    ky_copy.start()
    gx[0].start()

    @pl.when(jnp.logical_not(last))
    def _():
        chain(s, y).start()

    gc[0].start()
    gc[1].start()

    qbuf[y] = q_in[:, pl.ds(pl.multiple_of(y * gw, gw), gw)]

    def product(left, t, h):
        w_copy(t, h).wait()
        return dot(left, wbuf[2 * t + h], 1, 0)

    acc[...] = product(g_in[:, 0:half], t_own, 0)
    acc[...] += product(g_in[:, half:], t_own, 1)

    ky_copy.wait_recv()
    q_copy.start()

    @pl.when(jnp.logical_not(last))
    def _():
        chain(s, z).start()

    for h in range(2):
        gc[h].wait_recv()
        acc[...] += product(gbuf[t_core, h], t_core, h)
    gx[0].wait_send()
    gx[1].start()
    gx[0].wait_recv()
    gf[0].start()

    def arrive(k):
        for p in range(2):
            chain(k, p).wait_recv()

            @pl.when(jnp.logical_not(last))
            def _():
                chain(k, p).start()

    @pl.when(s >= 1)
    def _():
        arrive(s - 1)

    acc[...] += product(gbuf[t_x, 0], t_x, 0)
    gx[1].wait_recv()
    gf[1].start()

    @pl.when((s >= 2) & jnp.logical_not(last))
    def _():
        arrive(s - 2)

    acc[...] += product(gbuf[t_x, 1], t_x, 1)
    for h in range(2):
        gf[h].wait_recv()
        acc[...] += product(gbuf[t_f, h], t_f, h)
    usend[...] = acc[:, pl.ds(pl.multiple_of(z * gw, gw), gw)].astype(BF16)
    u_copy.start()
    ubuf[y] = acc[:, pl.ds(pl.multiple_of(y * gw, gw), gw)].astype(BF16)

    @pl.when(jnp.logical_not(last))
    def _():
        def body(i, carry):
            arrive(s - 3 - i)
            return carry

        lax.fori_loop(0, s - 2, body, 0)

    q_copy.wait_recv()

    mst[...] = jnp.full(mst.shape, -1e20, F32)
    lst[...] = jnp.zeros(lst.shape, F32)
    ot[...] = jnp.zeros(ot.shape, F32)
    ones[...] = jnp.zeros(ones.shape, F32)
    dq[...] = jnp.zeros(dq.shape, F32)

    def heads(ref, r):
        return ref[:, :, r * hs : (r + 1) * hs].reshape(pair, hs)

    def pieces(k):
        return kv[k, :, 0:rows, :].reshape(pair, hs), kv[k, :, rows : 2 * rows, :].reshape(pair, hs)

    def block(k):
        keys, values = pieces(k)
        begin = (s + 1) * pair - ones[0:1, :].astype(jnp.int32)
        qpos = s * pair + lax.broadcasted_iota(jnp.int32, (1, pair), 1)
        low = jnp.where(qpos < begin, 0, begin)
        kpos = k * pair + lax.broadcasted_iota(jnp.int32, (pair, pair), 0)
        return keys, values, (kpos <= qpos) & (kpos >= low)

    def scores(keys, allowed, r):
        sc = dot(keys, heads(qbuf, r), 1, 1) * (scale * LOG2E)
        return jnp.where(allowed, sc, -1e30)

    def statistics(i, carry):
        k = s - i

        @pl.when(last & (k < s - 1))
        def _():
            for p in range(2):
                chain(k, p).wait_recv()

        seg = kv[k, :, 2 * rows :, :].astype(F32).reshape(2 * SEG_ROWS, rows)
        count = jnp.sum(jnp.sum(seg, axis=0, keepdims=True), axis=1, keepdims=True) * (1.0 / SEG_ROWS)
        ones[...] += jnp.broadcast_to(count, ones.shape)
        keys, values, allowed = block(k)
        turned = values.T
        for r in range(RATIO):
            sc = scores(keys, allowed, r)
            if keep:
                kept[k, r] = sc
            old = mst[r : r + 1, :]
            new = jnp.maximum(old, jnp.max(sc, axis=0, keepdims=True))
            pr = jnp.exp2(sc - new)
            factor = jnp.exp2(old - new)
            mst[r : r + 1, :] = new
            lst[r : r + 1, :] = lst[r : r + 1, :] * factor + jnp.sum(pr, axis=0, keepdims=True)
            ot[r] = ot[r] * factor + dot(turned, pr.astype(BF16), 1, 0)
        return carry

    lax.fori_loop(0, s + 1, statistics, 0)
    u_copy.wait_recv()
    for r in range(RATIO):
        wst[r : r + 1, :] = jnp.sum(heads(ubuf, r).astype(F32).T * ot[r], axis=0, keepdims=True)
    mst[...] = mst[...] + jnp.log2(lst[...])
    wst[...] = wst[...] / lst[...]

    here = pl.ds(pl.multiple_of(y * rows, rows), rows)
    there = pl.ds(pl.multiple_of(z * rows, rows), rows)

    def back(k, p):
        return remote(rs.at[k, p], ret.at[k, p], ret_s.at[k, p], ret_r.at[k, p], up)

    def home(p):
        k = s - 1
        return (
            remote(rs.at[k, p, here], ret.at[k, p, here], ret_s.at[k, p], ret_r.at[k, p], up),
            remote(rs.at[k, p, there], retd.at[p], dia_s.at[p], dia_r.at[p], up_d),
        )

    def home_arrived(p):
        remote(rs.at[s, p, here], ret.at[s, p, here], ret_s.at[s, p], ret_r.at[s, p], up).wait_recv()
        remote(rs.at[s, p, there], retd.at[p], dia_s.at[p], dia_r.at[p], up_d).wait_recv()

    fin = [remote(fins.at[p], finr.at[p], fin_s.at[p], fin_r.at[p], sib) for p in range(2)]

    def gradients(k, carry):
        if keep:
            keys, values = pieces(k)
        else:
            keys, values, allowed = block(k)
        turned = keys.T
        dk = jnp.zeros((pair, hs), F32)
        dv = jnp.zeros((pair, hs), F32)
        for r in range(RATIO):
            sc = kept[k, r] if keep else scores(keys, allowed, r)
            dp = dot(values, heads(ubuf, r), 1, 1)
            pr = jnp.exp2(sc - mst[r : r + 1, :])
            ds = (pr * (dp - wst[r : r + 1, :])).astype(BF16)
            dv += dot(pr.astype(BF16), heads(ubuf, r), 1, 0)
            dk += dot(ds, heads(qbuf, r), 1, 0)
            dq[r] += dot(turned, ds, 1, 0)
        own[k, 0] = dk * scale
        own[k, 1] = dv

        @pl.when(last & (k < s))
        def _():
            for p in range(2):
                rs[k, p] = own[k, p].astype(BF16)

        @pl.when(last & (k >= 1) & (k < s))
        def _():
            for p in range(2):
                back(k - 1, p).wait_send()

        @pl.when(last & (k < s - 1))
        def _():
            for p in range(2):
                back(k, p).start()

        return carry

    lax.fori_loop(0, s + 1, gradients, 0)

    for r in range(RATIO):
        dqs[:, r * hs : (r + 1) * hs] = (
            dq[r, :, pl.ds(pl.multiple_of(z * rows, rows), rows)] * scale
        ).T.astype(BF16)
    dq_copy.start()
    for r in range(RATIO):
        q_out[:, pl.ds(pl.multiple_of(y * gw, gw) + r * hs, hs)] = (
            dq[r, :, pl.ds(pl.multiple_of(y * rows, rows), rows)] * scale
        ).T.astype(BF16)

    for p in range(2):
        fins[p] = own[s, p, there, :]
        fin[p].start()

    @pl.when(last & (s >= 1))
    def _():
        for p in range(2):
            for copy in home(p):
                copy.start()

    @pl.when(jnp.logical_not(last))
    def _():
        def body(k, carry):
            for p in range(2):
                back(k, p).wait_recv()
                rs[k, p] = (own[k, p] + ret[k, p].astype(F32)).astype(BF16)

                @pl.when(k < s - 1)
                def _():
                    back(k, p).start()

                @pl.when(k == s - 1)
                def _():
                    for copy in home(p):
                        copy.start()

            return carry

        lax.fori_loop(0, s, body, 0)

    dq_copy.wait_recv()
    q_out[:, pl.ds(pl.multiple_of(z * gw, gw), gw)] = dqr[...]
    mine = pl.ds(pl.multiple_of(y * hs, hs), hs)
    theirs = pl.ds(pl.multiple_of(z * hs, hs), hs)
    for p, out in enumerate((k_out, v_out)):
        fin[p].wait_recv()

        @pl.when(last)
        def _():
            out[:, mine] = own[s, p, here, :].astype(BF16)
            out[:, theirs] = finr[p].astype(BF16)

        @pl.when(jnp.logical_not(last))
        def _():
            home_arrived(p)
            out[:, mine] = (own[s, p, here, :] + ret[s, p, here, :].astype(F32)).astype(BF16)
            out[:, theirs] = (finr[p] + retd[p].astype(F32)).astype(BF16)

    for copy in (ky_copy, q_copy, u_copy, dq_copy, gx[1], *gc, *gf, *fin):
        copy.wait_send()

    @pl.when(jnp.logical_not(last))
    def _():
        def body(k, carry):
            for p in range(2):
                chain(k, p).wait_send()
            return carry

        lax.fori_loop(0, s + 1, body, 0)

    @pl.when(jnp.logical_not(last))
    def _():
        def body(k, carry):
            for p in range(2):
                back(k, p).wait_send()
            return carry

        lax.fori_loop(0, s - 1, body, 0)

    @pl.when(s >= 1)
    def _():
        for p in range(2):
            for copy in home(p):
                copy.wait_send()


def hand_over(a, b, c, x, y, z):
    x[...] = a[...]
    y[...] = b[...]
    z[...] = c[...]


def per_device(stages, queries, keys, values, grad_out, out_weight, segments):
    rows, wide = queries.shape
    depth = grad_out.shape[1]
    pair, hs, gw = 2 * rows, HEAD_SIZE, RATIO * HEAD_SIZE
    vmem = pl.BlockSpec(memory_space=pltpu.VMEM)
    dma = pltpu.SemaphoreType.DMA
    grads = pl.pallas_call(
        functools.partial(kernel, stages),
        out_shape=(
            jax.ShapeDtypeStruct(queries.shape, BF16),
            jax.ShapeDtypeStruct(keys.shape, BF16),
            jax.ShapeDtypeStruct(values.shape, BF16),
        ),
        in_specs=[vmem, vmem, vmem, vmem, pl.BlockSpec(memory_space=pl.ANY), vmem],
        out_specs=(vmem, vmem, vmem),
        scratch_shapes=[
            pltpu.VMEM((8, depth // 2, wide), BF16),
            pltpu.VMEM((4, 2, rows, depth // 2), BF16),
            pltpu.VMEM((rows, wide), F32),
            pltpu.VMEM((stages, 2, pair + SEG_ROWS, hs), BF16),
            pltpu.VMEM((pair + SEG_ROWS, hs), BF16),
            pltpu.VMEM((2, rows, gw), BF16),
            pltpu.VMEM((2, rows, gw), BF16),
            pltpu.VMEM((rows, gw), BF16),
            pltpu.VMEM((RATIO, pair), F32),
            pltpu.VMEM((RATIO, pair), F32),
            pltpu.VMEM((RATIO, pair), F32),
            pltpu.VMEM((8, pair), F32),
            pltpu.VMEM((RATIO, hs, pair), F32),
            pltpu.VMEM((stages if stages <= KEPT_STAGES else 1, RATIO, pair, pair), F32),
            pltpu.VMEM((RATIO, hs, pair), F32),
            pltpu.VMEM((rows, gw), BF16),
            pltpu.VMEM((rows, gw), BF16),
            pltpu.VMEM((stages, 2, pair, hs), F32),
            pltpu.VMEM((stages, 2, pair, hs), BF16),
            pltpu.VMEM((stages, 2, pair, hs), BF16),
            pltpu.VMEM((2, rows, hs), BF16),
            pltpu.VMEM((2, rows, hs), F32),
            pltpu.VMEM((2, rows, hs), F32),
            dma((8,)),
            dma((2,)), dma((2,)), dma((2,)), dma((2,)), dma((2,)), dma((2,)),
            dma((stages, 2)), dma((stages, 2)), dma((stages, 2)), dma((stages, 2)), dma((2,)), dma((2,)),
            dma((4,)), dma((4,)), dma((2,)), dma((2,)),
        ],
        compiler_params=pltpu.CompilerParams(
            collective_id=0, has_side_effects=True, vmem_limit_bytes=56 * 1024 * 1024
        ),
        name="attention_backward",
    )(queries, keys, values, grad_out, out_weight, segments.reshape(1, rows))
    return pl.pallas_call(
        hand_over,
        out_shape=tuple(jax.ShapeDtypeStruct(a.shape, a.dtype) for a in grads),
        in_specs=[vmem] * 3,
        out_specs=(vmem,) * 3,
        compiler_params=pltpu.CompilerParams(vmem_limit_bytes=56 * 1024 * 1024),
        name="hand_over",
    )(*grads)


def solution(mesh):
    in_specs = (
        P("ctx", "tp"),
        P("ctx", "tp"),
        P("ctx", "tp"),
        P("ctx", "tp"),
        P(None, "tp"),
        P("ctx"),
    )
    out_specs = (P("ctx", "tp"), P("ctx", "tp"), P("ctx", "tp"))
    return jax.shard_map(
        functools.partial(per_device, mesh.shape["ctx"] // 2),
        mesh=mesh, in_specs=in_specs, out_specs=out_specs, check_vma=False,
    )
```

```python
import functools

import jax
import jax.numpy as jnp
from jax import lax
from jax.experimental import pallas as pl
from jax.experimental.pallas import tpu as pltpu
from jax.sharding import PartitionSpec as P

QUERY_HEADS = 32
KEY_VALUE_HEADS = 8
HEAD_SIZE = 128
RATIO = QUERY_HEADS // KEY_VALUE_HEADS
SEG_ROWS = 16
KEPT_STAGES = 8
PARTS = 4
LOG2E = 1.4426950408889634
MESH = pl.DeviceIdType.MESH
F32 = jnp.float32
BF16 = jnp.bfloat16


def dot(a, b, ca, cb):
    return lax.dot_general(a, b, (((ca,), (cb,)), ((), ())), preferred_element_type=F32)


def kernel(
    stages, q_in, k_hbm, v_hbm, g_in, w_hbm, seg_hbm,
    q_out, k_out, v_out,
    k_in, v_in, seg_in, wbuf, gbuf, acc, kv, ky, qbuf, ubuf, usend, mst, lst, wst, ones, ot, kept,
    dq, dqs, dqr, own, rs, ret, retd, fins, finr,
    w_sem, in_sem, gx_s, gx_r, gc_s, gc_r, gf_s, gf_r, kv_s, kv_r, ret_s, ret_r, dia_s, dia_r,
    misc_s, misc_r, fin_s, fin_r,
):
    rows = k_hbm.shape[0]
    pair = 2 * rows
    hs = HEAD_SIZE
    gw = RATIO * hs
    keep = stages <= KEPT_STAGES
    part = g_in.shape[1] // PARTS
    scale = HEAD_SIZE ** -0.5
    ctx = lax.axis_index("ctx")
    tp = lax.axis_index("tp")
    s, y = ctx // 2, ctx % 2
    z = 1 - y
    x, c = tp // 2, tp % 2
    sib = (2 * s + z, tp)
    down = (2 * lax.rem(s + 1, stages) + y, tp)
    up = (2 * lax.rem(s + stages - 1, stages) + y, tp)
    down_d = (2 * lax.rem(s + 1, stages) + z, tp)
    up_d = (2 * lax.rem(s + stages - 1, stages) + z, tp)
    xnb = (ctx, 2 * (1 - x) + c)
    core = (ctx, 2 * x + 1 - c)
    t_own, t_core, t_x, t_f = tp, 2 * x + 1 - c, 2 * (1 - x) + c, 2 * (1 - x) + 1 - c

    barrier = pltpu.get_barrier_semaphore()
    for dev in (sib, down, up, down_d, up_d, xnb, core):
        pl.semaphore_signal(barrier, inc=1, device_id=dev, device_id_type=MESH)

    def remote(src, dst, a, b, dev):
        return pltpu.make_async_remote_copy(
            src_ref=src, dst_ref=dst, send_sem=a, recv_sem=b, device_id=dev, device_id_type=MESH
        )

    def w_copy(t, h):
        i = PARTS * t + h
        return pltpu.make_async_copy(w_hbm.at[pl.ds(i * part, part)], wbuf.at[i], w_sem.at[i])

    def g_part(h):
        return g_in.at[:, h * part : (h + 1) * part]

    own_q = pl.ds(pl.multiple_of(y * gw, gw), gw)
    loads = [
        pltpu.make_async_copy(src, dst, in_sem.at[i])
        for i, (src, dst) in enumerate(
            [(k_hbm, k_in), (v_hbm, v_in), (seg_hbm, seg_in), (q_in.at[:, own_q], qbuf.at[y])]
            + [(g_part(h), gbuf.at[t_own, h]) for h in range(PARTS)]
        )
    ]
    for copy in loads:
        copy.start()
    for t in (t_own, t_core, t_x, t_f):
        for h in range(PARTS):
            w_copy(t, h).start()
    for copy in loads[:3]:
        copy.wait()

    def fill(dst, g):
        cols = pl.ds(pl.multiple_of(g * hs, hs), hs)
        dst[0:rows, :] = k_in[:, cols]
        dst[rows : 2 * rows, :] = v_in[:, cols]
        dst[2 * rows :, :] = jnp.broadcast_to(seg_in[...].astype(F32), (SEG_ROWS, rows)).astype(BF16)

    fill(kv.at[s, y], y)
    fill(ky, z)

    pl.semaphore_wait(barrier, 7)

    def chain(k, p):
        return remote(kv.at[k, p], kv.at[k, p], kv_s.at[k, p], kv_r.at[k, p], down)

    ky_copy = remote(ky, kv.at[s, y], misc_s.at[0], misc_r.at[0], sib)
    q_copy = remote(
        q_in.at[:, pl.ds(pl.multiple_of(z * gw, gw), gw)], qbuf.at[y], misc_s.at[1], misc_r.at[1], sib
    )
    u_copy = remote(usend, ubuf.at[y], misc_s.at[2], misc_r.at[2], sib)
    dq_copy = remote(dqs, dqr, misc_s.at[3], misc_r.at[3], sib)
    parts = range(PARTS)
    gx = [remote(g_part(h), gbuf.at[t_own, h], gx_s.at[h], gx_r.at[h], xnb) for h in parts]
    gc = [remote(g_part(h), gbuf.at[t_own, h], gc_s.at[h], gc_r.at[h], core) for h in parts]
    gf = [remote(gbuf.at[t_x, h], gbuf.at[t_x, h], gf_s.at[h], gf_r.at[h], core) for h in parts]
    last = s == stages - 1

    ky_copy.start()
    gx[0].start()
    gx[1].start()

    @pl.when(jnp.logical_not(last))
    def _():
        chain(s, y).start()

    for copy in gc:
        copy.start()

    def product(t, h):
        w_copy(t, h).wait()
        return dot(gbuf[t, h], wbuf[PARTS * t + h], 1, 0)

    for copy in loads[3:]:
        copy.wait()
    acc[...] = product(t_own, 0)
    for h in range(1, PARTS):
        acc[...] += product(t_own, h)

    ky_copy.wait_recv()
    q_copy.start()

    @pl.when(jnp.logical_not(last))
    def _():
        chain(s, z).start()

    gx[0].wait_send()
    gx[2].start()
    for h in parts:
        gc[h].wait_recv()
        acc[...] += product(t_core, h)
    gx[1].wait_send()
    gx[3].start()

    def arrive(k):
        for p in range(2):
            chain(k, p).wait_recv()

            @pl.when(jnp.logical_not(last))
            def _():
                chain(k, p).start()

    for h in parts:
        gx[h].wait_recv()
        gf[h].start()
        if h == 0:
            @pl.when(s >= 1)
            def _():
                arrive(s - 1)

        if h == PARTS - 1:
            @pl.when((s >= 2) & jnp.logical_not(last))
            def _():
                arrive(s - 2)

        acc[...] += product(t_x, h)
    for h in parts:
        gf[h].wait_recv()
        acc[...] += product(t_f, h)
    usend[...] = acc[:, pl.ds(pl.multiple_of(z * gw, gw), gw)].astype(BF16)
    u_copy.start()
    ubuf[y] = acc[:, pl.ds(pl.multiple_of(y * gw, gw), gw)].astype(BF16)

    @pl.when(jnp.logical_not(last))
    def _():
        def body(i, carry):
            arrive(s - 3 - i)
            return carry

        lax.fori_loop(0, s - 2, body, 0)

    q_copy.wait_recv()

    mst[...] = jnp.full(mst.shape, -1e20, F32)
    lst[...] = jnp.zeros(lst.shape, F32)
    ot[...] = jnp.zeros(ot.shape, F32)
    ones[...] = jnp.zeros(ones.shape, F32)
    dq[...] = jnp.zeros(dq.shape, F32)

    def heads(ref, r):
        return ref[:, :, r * hs : (r + 1) * hs].reshape(pair, hs)

    def pieces(k):
        return kv[k, :, 0:rows, :].reshape(pair, hs), kv[k, :, rows : 2 * rows, :].reshape(pair, hs)

    def block(k):
        keys, values = pieces(k)
        begin = (s + 1) * pair - ones[0:1, :].astype(jnp.int32)
        qpos = s * pair + lax.broadcasted_iota(jnp.int32, (1, pair), 1)
        low = jnp.where(qpos < begin, 0, begin)
        kpos = k * pair + lax.broadcasted_iota(jnp.int32, (pair, pair), 0)
        return keys, values, (kpos <= qpos) & (kpos >= low)

    def scores(keys, allowed, r):
        sc = dot(keys, heads(qbuf, r), 1, 1) * (scale * LOG2E)
        return jnp.where(allowed, sc, -1e30)

    def statistics(i, carry):
        k = s - i

        @pl.when(last & (k < s - 1))
        def _():
            for p in range(2):
                chain(k, p).wait_recv()

        seg = kv[k, :, 2 * rows :, :].astype(F32).reshape(2 * SEG_ROWS, rows)
        count = jnp.sum(jnp.sum(seg, axis=0, keepdims=True), axis=1, keepdims=True) * (1.0 / SEG_ROWS)
        ones[...] += jnp.broadcast_to(count, ones.shape)
        keys, values, allowed = block(k)
        turned = values.T
        for r in range(RATIO):
            sc = scores(keys, allowed, r)
            if keep:
                kept[k, r] = sc
            old = mst[r : r + 1, :]
            new = jnp.maximum(old, jnp.max(sc, axis=0, keepdims=True))
            pr = jnp.exp2(sc - new)
            factor = jnp.exp2(old - new)
            mst[r : r + 1, :] = new
            lst[r : r + 1, :] = lst[r : r + 1, :] * factor + jnp.sum(pr, axis=0, keepdims=True)
            ot[r] = ot[r] * factor + dot(turned, pr.astype(BF16), 1, 0)
        return carry

    lax.fori_loop(0, s + 1, statistics, 0)
    u_copy.wait_recv()
    for r in range(RATIO):
        wst[r : r + 1, :] = jnp.sum(heads(ubuf, r).astype(F32).T * ot[r], axis=0, keepdims=True)
    mst[...] = mst[...] + jnp.log2(lst[...])
    wst[...] = wst[...] / lst[...]

    here = pl.ds(pl.multiple_of(y * rows, rows), rows)
    there = pl.ds(pl.multiple_of(z * rows, rows), rows)

    def back(k, p):
        return remote(rs.at[k, p], ret.at[k, p], ret_s.at[k, p], ret_r.at[k, p], up)

    def home(p):
        k = s - 1
        return (
            remote(rs.at[k, p, here], ret.at[k, p, here], ret_s.at[k, p], ret_r.at[k, p], up),
            remote(rs.at[k, p, there], retd.at[p], dia_s.at[p], dia_r.at[p], up_d),
        )

    def home_arrived(p):
        remote(rs.at[s, p, here], ret.at[s, p, here], ret_s.at[s, p], ret_r.at[s, p], up).wait_recv()
        remote(rs.at[s, p, there], retd.at[p], dia_s.at[p], dia_r.at[p], up_d).wait_recv()

    fin = [remote(fins.at[p], finr.at[p], fin_s.at[p], fin_r.at[p], sib) for p in range(2)]

    def gradients(k, carry):
        if keep:
            keys, values = pieces(k)
        else:
            keys, values, allowed = block(k)
        turned = keys.T
        dk = jnp.zeros((pair, hs), F32)
        dv = jnp.zeros((pair, hs), F32)
        for r in range(RATIO):
            sc = kept[k, r] if keep else scores(keys, allowed, r)
            dp = dot(values, heads(ubuf, r), 1, 1)
            pr = jnp.exp2(sc - mst[r : r + 1, :])
            ds = (pr * (dp - wst[r : r + 1, :])).astype(BF16)
            dv += dot(pr.astype(BF16), heads(ubuf, r), 1, 0)
            dk += dot(ds, heads(qbuf, r), 1, 0)
            dq[r] += dot(turned, ds, 1, 0)
        own[k, 0] = dk * scale
        own[k, 1] = dv

        @pl.when(last & (k < s))
        def _():
            for p in range(2):
                rs[k, p] = own[k, p].astype(BF16)

        @pl.when(last & (k < s - 1))
        def _():
            for p in range(2):
                @pl.when(k >= 1)
                def _():
                    back(k - 1, p).wait_send()

                back(k, p).start()

        return carry

    lax.fori_loop(0, s + 1, gradients, 0)

    for r in range(RATIO):
        dqs[:, r * hs : (r + 1) * hs] = (
            dq[r, :, pl.ds(pl.multiple_of(z * rows, rows), rows)] * scale
        ).T.astype(BF16)
    dq_copy.start()
    for r in range(RATIO):
        q_out[:, pl.ds(pl.multiple_of(y * gw, gw) + r * hs, hs)] = (
            dq[r, :, pl.ds(pl.multiple_of(y * rows, rows), rows)] * scale
        ).T.astype(BF16)

    for p in range(2):
        fins[p] = own[s, p, there, :]
        fin[p].start()

    @pl.when(last & (s >= 1))
    def _():
        for p in range(2):
            @pl.when(s >= 2)
            def _():
                back(s - 2, p).wait_send()

            for copy in home(p):
                copy.start()

    @pl.when(jnp.logical_not(last))
    def _():
        def body(k, carry):
            for p in range(2):
                back(k, p).wait_recv()
                rs[k, p] = (own[k, p] + ret[k, p].astype(F32)).astype(BF16)

                @pl.when(k < s - 1)
                def _():
                    back(k, p).start()

                @pl.when(k == s - 1)
                def _():
                    for copy in home(p):
                        copy.start()

            return carry

        lax.fori_loop(0, s, body, 0)

    dq_copy.wait_recv()
    q_out[:, pl.ds(pl.multiple_of(z * gw, gw), gw)] = dqr[...]
    mine = pl.ds(pl.multiple_of(y * hs, hs), hs)
    theirs = pl.ds(pl.multiple_of(z * hs, hs), hs)
    for p, out in enumerate((k_out, v_out)):
        fin[p].wait_recv()

        @pl.when(last)
        def _():
            out[:, mine] = own[s, p, here, :].astype(BF16)
            out[:, theirs] = finr[p].astype(BF16)

        @pl.when(jnp.logical_not(last))
        def _():
            home_arrived(p)
            out[:, mine] = (own[s, p, here, :] + ret[s, p, here, :].astype(F32)).astype(BF16)
            out[:, theirs] = (finr[p] + retd[p].astype(F32)).astype(BF16)

    for copy in (ky_copy, q_copy, u_copy, dq_copy, gx[2], gx[3], *gc, *gf, *fin):
        copy.wait_send()

    @pl.when(jnp.logical_not(last))
    def _():
        def body(k, carry):
            for p in range(2):
                chain(k, p).wait_send()
            return carry

        lax.fori_loop(0, s + 1, body, 0)

    @pl.when(jnp.logical_not(last))
    def _():
        def body(k, carry):
            for p in range(2):
                back(k, p).wait_send()
            return carry

        lax.fori_loop(0, s - 1, body, 0)

    @pl.when(s >= 1)
    def _():
        for p in range(2):
            for copy in home(p):
                copy.wait_send()


def hand_over(a, b, c, x, y, z):
    x[...] = a[...]
    y[...] = b[...]
    z[...] = c[...]


def per_device(stages, queries, keys, values, grad_out, out_weight, segments):
    rows, wide = queries.shape
    depth = grad_out.shape[1]
    pair, hs, gw = 2 * rows, HEAD_SIZE, RATIO * HEAD_SIZE
    vmem = pl.BlockSpec(memory_space=pltpu.VMEM)
    dma = pltpu.SemaphoreType.DMA
    grads = pl.pallas_call(
        functools.partial(kernel, stages),
        out_shape=(
            jax.ShapeDtypeStruct(queries.shape, BF16),
            jax.ShapeDtypeStruct(keys.shape, BF16),
            jax.ShapeDtypeStruct(values.shape, BF16),
        ),
        in_specs=[pl.BlockSpec(memory_space=pl.ANY)] * 6,
        out_specs=(vmem, vmem, vmem),
        scratch_shapes=[
            pltpu.VMEM(keys.shape, BF16),
            pltpu.VMEM(values.shape, BF16),
            pltpu.VMEM((1, rows), jnp.int32),
            pltpu.VMEM((4 * PARTS, depth // PARTS, wide), BF16),
            pltpu.VMEM((4, PARTS, rows, depth // PARTS), BF16),
            pltpu.VMEM((rows, wide), F32),
            pltpu.VMEM((stages, 2, pair + SEG_ROWS, hs), BF16),
            pltpu.VMEM((pair + SEG_ROWS, hs), BF16),
            pltpu.VMEM((2, rows, gw), BF16),
            pltpu.VMEM((2, rows, gw), BF16),
            pltpu.VMEM((rows, gw), BF16),
            pltpu.VMEM((RATIO, pair), F32),
            pltpu.VMEM((RATIO, pair), F32),
            pltpu.VMEM((RATIO, pair), F32),
            pltpu.VMEM((8, pair), F32),
            pltpu.VMEM((RATIO, hs, pair), F32),
            pltpu.VMEM((stages if stages <= KEPT_STAGES else 1, RATIO, pair, pair), F32),
            pltpu.VMEM((RATIO, hs, pair), F32),
            pltpu.VMEM((rows, gw), BF16),
            pltpu.VMEM((rows, gw), BF16),
            pltpu.VMEM((stages, 2, pair, hs), F32),
            pltpu.VMEM((stages, 2, pair, hs), BF16),
            pltpu.VMEM((stages, 2, pair, hs), BF16),
            pltpu.VMEM((2, rows, hs), BF16),
            pltpu.VMEM((2, rows, hs), F32),
            pltpu.VMEM((2, rows, hs), F32),
            dma((4 * PARTS,)), dma((4 + PARTS,)),
            *[dma((PARTS,))] * 6,
            dma((stages, 2)), dma((stages, 2)), dma((stages, 2)), dma((stages, 2)), dma((2,)), dma((2,)),
            dma((4,)), dma((4,)), dma((2,)), dma((2,)),
        ],
        compiler_params=pltpu.CompilerParams(
            collective_id=0, has_side_effects=True, vmem_limit_bytes=56 * 1024 * 1024
        ),
        name="attention_backward",
    )(queries, keys, values, grad_out, out_weight, segments.reshape(1, rows))
    return pl.pallas_call(
        hand_over,
        out_shape=tuple(jax.ShapeDtypeStruct(a.shape, a.dtype) for a in grads),
        in_specs=[vmem] * 3,
        out_specs=(vmem,) * 3,
        compiler_params=pltpu.CompilerParams(vmem_limit_bytes=56 * 1024 * 1024),
        name="hand_over",
    )(*grads)


def solution(mesh):
    in_specs = (
        P("ctx", "tp"),
        P("ctx", "tp"),
        P("ctx", "tp"),
        P("ctx", "tp"),
        P(None, "tp"),
        P("ctx"),
    )
    out_specs = (P("ctx", "tp"), P("ctx", "tp"), P("ctx", "tp"))
    return jax.shard_map(
        functools.partial(per_device, mesh.shape["ctx"] // 2),
        mesh=mesh, in_specs=in_specs, out_specs=out_specs, check_vma=False,
    )
```

```python
import functools

import jax
import jax.numpy as jnp
from jax import lax
from jax.experimental import pallas as pl
from jax.experimental.pallas import tpu as pltpu
from jax.sharding import PartitionSpec as P

QUERY_HEADS = 32
KEY_VALUE_HEADS = 8
HEAD_SIZE = 128
RATIO = QUERY_HEADS // KEY_VALUE_HEADS
SEG_ROWS = 16
KEPT_STAGES = 8
PARTS = 4
LOG2E = 1.4426950408889634
MESH = pl.DeviceIdType.MESH
F32 = jnp.float32
BF16 = jnp.bfloat16


def dot(a, b, ca, cb):
    return lax.dot_general(a, b, (((ca,), (cb,)), ((), ())), preferred_element_type=F32)


def kernel(
    stages, q_in, k_hbm, v_hbm, g_in, w_hbm, seg_hbm,
    q_out, k_out, v_out,
    k_in, v_in, seg_in, wbuf, gbuf, acc, kv, ky, qbuf, ubuf, usend, mst, lst, wst, ones, ot, kept,
    dq, dqs, dqr, own, rs, ret, retd, fins, finr,
    w_sem, in_sem, gx_s, gx_r, gc_s, gc_r, gf_s, gf_r, kv_s, kv_r, ret_s, ret_r, dia_s, dia_r,
    misc_s, misc_r, fin_s, fin_r,
):
    rows = k_hbm.shape[0]
    pair = 2 * rows
    hs = HEAD_SIZE
    gw = RATIO * hs
    keep = stages <= KEPT_STAGES
    part = g_in.shape[1] // PARTS
    scale = HEAD_SIZE ** -0.5
    ctx = lax.axis_index("ctx")
    tp = lax.axis_index("tp")
    s, y = ctx // 2, ctx % 2
    z = 1 - y
    x, c = tp // 2, tp % 2
    sib = (2 * s + z, tp)
    down = (2 * lax.rem(s + 1, stages) + y, tp)
    up = (2 * lax.rem(s + stages - 1, stages) + y, tp)
    down_d = (2 * lax.rem(s + 1, stages) + z, tp)
    up_d = (2 * lax.rem(s + stages - 1, stages) + z, tp)
    xnb = (ctx, 2 * (1 - x) + c)
    core = (ctx, 2 * x + 1 - c)
    t_own, t_core, t_x, t_f = tp, 2 * x + 1 - c, 2 * (1 - x) + c, 2 * (1 - x) + 1 - c

    barrier = pltpu.get_barrier_semaphore()
    for dev in (sib, down, up, down_d, up_d, xnb, core):
        pl.semaphore_signal(barrier, inc=1, device_id=dev, device_id_type=MESH)

    def remote(src, dst, a, b, dev):
        return pltpu.make_async_remote_copy(
            src_ref=src, dst_ref=dst, send_sem=a, recv_sem=b, device_id=dev, device_id_type=MESH
        )

    def w_copy(t, h):
        i = PARTS * t + h
        return pltpu.make_async_copy(w_hbm.at[pl.ds(i * part, part)], wbuf.at[i], w_sem.at[i])

    def g_part(h):
        return g_in.at[:, h * part : (h + 1) * part]

    own_q = pl.ds(pl.multiple_of(y * gw, gw), gw)
    loads = [
        pltpu.make_async_copy(src, dst, in_sem.at[i])
        for i, (src, dst) in enumerate(
            [(k_hbm, k_in), (v_hbm, v_in), (seg_hbm, seg_in), (q_in.at[:, own_q], qbuf.at[y])]
            + [(g_part(h), gbuf.at[t_own, h]) for h in range(PARTS)]
        )
    ]
    for copy in loads:
        copy.start()
    for t in (t_own, t_core, t_x, t_f):
        for h in range(PARTS):
            w_copy(t, h).start()
    for copy in loads[:3]:
        copy.wait()

    def fill(dst, g):
        cols = pl.ds(pl.multiple_of(g * hs, hs), hs)
        dst[0:rows, :] = k_in[:, cols]
        dst[rows : 2 * rows, :] = v_in[:, cols]
        dst[2 * rows :, :] = jnp.broadcast_to(seg_in[...].astype(F32), (SEG_ROWS, rows)).astype(BF16)

    fill(kv.at[s, y], y)
    fill(ky, z)

    pl.semaphore_wait(barrier, 7)

    def chain(k, p):
        return remote(kv.at[k, p], kv.at[k, p], kv_s.at[k, p], kv_r.at[k, p], down)

    ky_copy = remote(ky, kv.at[s, y], misc_s.at[0], misc_r.at[0], sib)
    q_copy = remote(
        q_in.at[:, pl.ds(pl.multiple_of(z * gw, gw), gw)], qbuf.at[y], misc_s.at[1], misc_r.at[1], sib
    )
    u_copy = remote(usend, ubuf.at[y], misc_s.at[2], misc_r.at[2], sib)
    dq_copy = remote(dqs, dqr, misc_s.at[3], misc_r.at[3], sib)
    parts = range(PARTS)
    gx = [remote(g_part(h), gbuf.at[t_own, h], gx_s.at[h], gx_r.at[h], xnb) for h in parts]
    gc = [remote(g_part(h), gbuf.at[t_own, h], gc_s.at[h], gc_r.at[h], core) for h in parts]
    gf = [remote(gbuf.at[t_x, h], gbuf.at[t_x, h], gf_s.at[h], gf_r.at[h], core) for h in parts]
    last = s == stages - 1

    ky_copy.start()
    for copy in gx:
        copy.start()

    @pl.when(jnp.logical_not(last))
    def _():
        chain(s, y).start()

    for copy in gc:
        copy.start()

    def product(t, h):
        w_copy(t, h).wait()
        return dot(gbuf[t, h], wbuf[PARTS * t + h], 1, 0)

    for copy in loads[3:]:
        copy.wait()
    acc[...] = product(t_own, 0)
    for h in range(1, PARTS):
        acc[...] += product(t_own, h)

    ky_copy.wait_recv()
    q_copy.start()

    @pl.when(jnp.logical_not(last))
    def _():
        chain(s, z).start()

    for h in parts:
        gc[h].wait_recv()
        acc[...] += product(t_core, h)

    def arrive_part(k, p):
        chain(k, p).wait_recv()

        @pl.when(jnp.logical_not(last))
        def _():
            chain(k, p).start()

    def arrive(k):
        for p in range(2):
            arrive_part(k, p)

    for h in parts:
        gx[h].wait_recv()
        gf[h].start()
        if h in (0, 2):
            @pl.when(s >= 1)
            def _():
                arrive_part(s - 1, z if h else y)

        if h == PARTS - 1:
            @pl.when((s >= 2) & jnp.logical_not(last))
            def _():
                arrive(s - 2)

        acc[...] += product(t_x, h)

    mst[...] = jnp.full(mst.shape, -1e20, F32)
    lst[...] = jnp.zeros(lst.shape, F32)
    ot[...] = jnp.zeros(ot.shape, F32)
    ones[...] = jnp.zeros(ones.shape, F32)
    dq[...] = jnp.zeros(dq.shape, F32)

    def heads(ref, r):
        return ref[:, :, r * hs : (r + 1) * hs].reshape(pair, hs)

    def pieces(k):
        return kv[k, :, 0:rows, :].reshape(pair, hs), kv[k, :, rows : 2 * rows, :].reshape(pair, hs)

    def block(k):
        keys, values = pieces(k)
        begin = (s + 1) * pair - ones[0:1, :].astype(jnp.int32)
        qpos = s * pair + lax.broadcasted_iota(jnp.int32, (1, pair), 1)
        low = jnp.where(qpos < begin, 0, begin)
        kpos = k * pair + lax.broadcasted_iota(jnp.int32, (pair, pair), 0)
        return keys, values, (kpos <= qpos) & (kpos >= low)

    def scores(keys, allowed, r):
        sc = dot(keys, heads(qbuf, r), 1, 1) * (scale * LOG2E)
        return jnp.where(allowed, sc, -1e30)

    def statistics(i, carry):
        k = s - i

        @pl.when(last & (k < s - 1))
        def _():
            for p in range(2):
                chain(k, p).wait_recv()

        seg = kv[k, :, 2 * rows :, :].astype(F32).reshape(2 * SEG_ROWS, rows)
        count = jnp.sum(jnp.sum(seg, axis=0, keepdims=True), axis=1, keepdims=True) * (1.0 / SEG_ROWS)
        ones[...] += jnp.broadcast_to(count, ones.shape)
        keys, values, allowed = block(k)
        turned = values.T
        for r in range(RATIO):
            sc = scores(keys, allowed, r)
            if keep:
                kept[k, r] = sc
            old = mst[r : r + 1, :]
            new = jnp.maximum(old, jnp.max(sc, axis=0, keepdims=True))
            pr = jnp.exp2(sc - new)
            factor = jnp.exp2(old - new)
            mst[r : r + 1, :] = new
            lst[r : r + 1, :] = lst[r : r + 1, :] * factor + jnp.sum(pr, axis=0, keepdims=True)
            ot[r] = ot[r] * factor + dot(turned, pr.astype(BF16), 1, 0)
        return carry

    for h in parts:
        if h == PARTS - 1:
            q_copy.wait_recv()
            statistics(0, 0)
        gf[h].wait_recv()
        acc[...] += product(t_f, h)
    usend[...] = acc[:, pl.ds(pl.multiple_of(z * gw, gw), gw)].astype(BF16)
    u_copy.start()
    ubuf[y] = acc[:, pl.ds(pl.multiple_of(y * gw, gw), gw)].astype(BF16)

    @pl.when(jnp.logical_not(last))
    def _():
        def body(i, carry):
            arrive(s - 3 - i)
            return carry

        lax.fori_loop(0, s - 2, body, 0)

    lax.fori_loop(1, s + 1, statistics, 0)
    u_copy.wait_recv()
    for r in range(RATIO):
        wst[r : r + 1, :] = jnp.sum(heads(ubuf, r).astype(F32).T * ot[r], axis=0, keepdims=True)
    mst[...] = mst[...] + jnp.log2(lst[...])
    wst[...] = wst[...] / lst[...]

    here = pl.ds(pl.multiple_of(y * rows, rows), rows)
    there = pl.ds(pl.multiple_of(z * rows, rows), rows)

    def back(k, p):
        return remote(rs.at[k, p], ret.at[k, p], ret_s.at[k, p], ret_r.at[k, p], up)

    def home(p):
        k = s - 1
        return (
            remote(rs.at[k, p, here], ret.at[k, p, here], ret_s.at[k, p], ret_r.at[k, p], up),
            remote(rs.at[k, p, there], retd.at[p], dia_s.at[p], dia_r.at[p], up_d),
        )

    def home_arrived(p):
        remote(rs.at[s, p, here], ret.at[s, p, here], ret_s.at[s, p], ret_r.at[s, p], up).wait_recv()
        remote(rs.at[s, p, there], retd.at[p], dia_s.at[p], dia_r.at[p], up_d).wait_recv()

    fin = [remote(fins.at[p], finr.at[p], fin_s.at[p], fin_r.at[p], sib) for p in range(2)]

    def gradients(k, carry):
        if keep:
            keys, values = pieces(k)
        else:
            keys, values, allowed = block(k)
        turned = keys.T
        dk = jnp.zeros((pair, hs), F32)
        dv = jnp.zeros((pair, hs), F32)
        for r in range(RATIO):
            sc = kept[k, r] if keep else scores(keys, allowed, r)
            dp = dot(values, heads(ubuf, r), 1, 1)
            pr = jnp.exp2(sc - mst[r : r + 1, :])
            ds = (pr * (dp - wst[r : r + 1, :])).astype(BF16)
            dv += dot(pr.astype(BF16), heads(ubuf, r), 1, 0)
            dk += dot(ds, heads(qbuf, r), 1, 0)
            dq[r] += dot(turned, ds, 1, 0)
        own[k, 0] = dk * scale
        own[k, 1] = dv

        @pl.when(last & (k < s))
        def _():
            for p in range(2):
                rs[k, p] = own[k, p].astype(BF16)

        @pl.when(last & (k < s - 1))
        def _():
            for p in range(2):
                back(k, p).start()

        @pl.when(last & (k == s - 1))
        def _():
            for p in range(2):
                for copy in home(p):
                    copy.start()

        return carry

    lax.fori_loop(0, s + 1, gradients, 0)

    for r in range(RATIO):
        dqs[:, r * hs : (r + 1) * hs] = (
            dq[r, :, pl.ds(pl.multiple_of(z * rows, rows), rows)] * scale
        ).T.astype(BF16)
    dq_copy.start()
    for r in range(RATIO):
        q_out[:, pl.ds(pl.multiple_of(y * gw, gw) + r * hs, hs)] = (
            dq[r, :, pl.ds(pl.multiple_of(y * rows, rows), rows)] * scale
        ).T.astype(BF16)

    for p in range(2):
        fins[p] = own[s, p, there, :]
        fin[p].start()

    @pl.when(jnp.logical_not(last))
    def _():
        def body(k, carry):
            for p in range(2):
                back(k, p).wait_recv()
                rs[k, p] = (own[k, p] + ret[k, p].astype(F32)).astype(BF16)

                @pl.when(k < s - 1)
                def _():
                    back(k, p).start()

                @pl.when(k == s - 1)
                def _():
                    for copy in home(p):
                        copy.start()

            return carry

        lax.fori_loop(0, s, body, 0)

    dq_copy.wait_recv()
    q_out[:, pl.ds(pl.multiple_of(z * gw, gw), gw)] = dqr[...]
    mine = pl.ds(pl.multiple_of(y * hs, hs), hs)
    theirs = pl.ds(pl.multiple_of(z * hs, hs), hs)
    for p, out in enumerate((k_out, v_out)):
        fin[p].wait_recv()

        @pl.when(last)
        def _():
            out[:, mine] = own[s, p, here, :].astype(BF16)
            out[:, theirs] = finr[p].astype(BF16)

        @pl.when(jnp.logical_not(last))
        def _():
            home_arrived(p)
            out[:, mine] = (own[s, p, here, :] + ret[s, p, here, :].astype(F32)).astype(BF16)
            out[:, theirs] = (finr[p] + retd[p].astype(F32)).astype(BF16)

    for copy in (ky_copy, q_copy, u_copy, dq_copy, *gx, *gc, *gf, *fin):
        copy.wait_send()

    @pl.when(jnp.logical_not(last))
    def _():
        def body(k, carry):
            for p in range(2):
                chain(k, p).wait_send()
            return carry

        lax.fori_loop(0, s + 1, body, 0)

    def drain(k, carry):
        for p in range(2):
            back(k, p).wait_send()
        return carry

    lax.fori_loop(0, s - 1, drain, 0)

    @pl.when(s >= 1)
    def _():
        for p in range(2):
            for copy in home(p):
                copy.wait_send()


def hand_over(a, b, c, x, y, z):
    x[...] = a[...]
    y[...] = b[...]
    z[...] = c[...]


def per_device(stages, queries, keys, values, grad_out, out_weight, segments):
    rows, wide = queries.shape
    depth = grad_out.shape[1]
    pair, hs, gw = 2 * rows, HEAD_SIZE, RATIO * HEAD_SIZE
    vmem = pl.BlockSpec(memory_space=pltpu.VMEM)
    dma = pltpu.SemaphoreType.DMA
    grads = pl.pallas_call(
        functools.partial(kernel, stages),
        out_shape=(
            jax.ShapeDtypeStruct(queries.shape, BF16),
            jax.ShapeDtypeStruct(keys.shape, BF16),
            jax.ShapeDtypeStruct(values.shape, BF16),
        ),
        in_specs=[pl.BlockSpec(memory_space=pl.ANY)] * 6,
        out_specs=(vmem, vmem, vmem),
        scratch_shapes=[
            pltpu.VMEM(keys.shape, BF16),
            pltpu.VMEM(values.shape, BF16),
            pltpu.VMEM((1, rows), jnp.int32),
            pltpu.VMEM((4 * PARTS, depth // PARTS, wide), BF16),
            pltpu.VMEM((4, PARTS, rows, depth // PARTS), BF16),
            pltpu.VMEM((rows, wide), F32),
            pltpu.VMEM((stages, 2, pair + SEG_ROWS, hs), BF16),
            pltpu.VMEM((pair + SEG_ROWS, hs), BF16),
            pltpu.VMEM((2, rows, gw), BF16),
            pltpu.VMEM((2, rows, gw), BF16),
            pltpu.VMEM((rows, gw), BF16),
            pltpu.VMEM((RATIO, pair), F32),
            pltpu.VMEM((RATIO, pair), F32),
            pltpu.VMEM((RATIO, pair), F32),
            pltpu.VMEM((8, pair), F32),
            pltpu.VMEM((RATIO, hs, pair), F32),
            pltpu.VMEM((stages if stages <= KEPT_STAGES else 1, RATIO, pair, pair), F32),
            pltpu.VMEM((RATIO, hs, pair), F32),
            pltpu.VMEM((rows, gw), BF16),
            pltpu.VMEM((rows, gw), BF16),
            pltpu.VMEM((stages, 2, pair, hs), F32),
            pltpu.VMEM((stages, 2, pair, hs), BF16),
            pltpu.VMEM((stages, 2, pair, hs), BF16),
            pltpu.VMEM((2, rows, hs), BF16),
            pltpu.VMEM((2, rows, hs), F32),
            pltpu.VMEM((2, rows, hs), F32),
            dma((4 * PARTS,)), dma((4 + PARTS,)),
            *[dma((PARTS,))] * 6,
            dma((stages, 2)), dma((stages, 2)), dma((stages, 2)), dma((stages, 2)), dma((2,)), dma((2,)),
            dma((4,)), dma((4,)), dma((2,)), dma((2,)),
        ],
        compiler_params=pltpu.CompilerParams(
            collective_id=0, has_side_effects=True, vmem_limit_bytes=56 * 1024 * 1024
        ),
        name="attention_backward",
    )(queries, keys, values, grad_out, out_weight, segments.reshape(1, rows))
    return pl.pallas_call(
        hand_over,
        out_shape=tuple(jax.ShapeDtypeStruct(a.shape, a.dtype) for a in grads),
        in_specs=[vmem] * 3,
        out_specs=(vmem,) * 3,
        compiler_params=pltpu.CompilerParams(vmem_limit_bytes=56 * 1024 * 1024),
        name="hand_over",
    )(*grads)


def solution(mesh):
    in_specs = (
        P("ctx", "tp"),
        P("ctx", "tp"),
        P("ctx", "tp"),
        P("ctx", "tp"),
        P(None, "tp"),
        P("ctx"),
    )
    out_specs = (P("ctx", "tp"), P("ctx", "tp"), P("ctx", "tp"))
    return jax.shard_map(
        functools.partial(per_device, mesh.shape["ctx"] // 2),
        mesh=mesh, in_specs=in_specs, out_specs=out_specs, check_vma=False,
    )
```

```python
import functools

import jax
import jax.numpy as jnp
from jax import lax
from jax.experimental import pallas as pl
from jax.experimental.pallas import tpu as pltpu
from jax.sharding import PartitionSpec as P

QUERY_HEADS = 32
KEY_VALUE_HEADS = 8
HEAD_SIZE = 128
RATIO = QUERY_HEADS // KEY_VALUE_HEADS
SEG_ROWS = 16
KEPT_STAGES = 8
PARTS = 4
LOG2E = 1.4426950408889634
MESH = pl.DeviceIdType.MESH
F32 = jnp.float32
BF16 = jnp.bfloat16


def dot(a, b, ca, cb):
    return lax.dot_general(a, b, (((ca,), (cb,)), ((), ())), preferred_element_type=F32)


def kernel(
    stages, q_in, k_hbm, v_hbm, g_in, w_hbm, seg_hbm,
    q_out, k_out, v_out,
    k_in, v_in, seg_in, wbuf, gbuf, acc, kv, ky, qbuf, ubuf, usend, mst, lst, wst, ones, ot, kept,
    dq, dqs, dqr, own, rs, ret, retd, fins, finr,
    w_sem, in_sem, gx_s, gx_r, gc_s, gc_r, gf_s, gf_r, kv_s, kv_r, ret_s, ret_r, dia_s, dia_r,
    misc_s, misc_r, fin_s, fin_r,
):
    rows = k_hbm.shape[0]
    pair = 2 * rows
    hs = HEAD_SIZE
    gw = RATIO * hs
    keep = stages <= KEPT_STAGES
    part = g_in.shape[1] // PARTS
    scale = HEAD_SIZE ** -0.5
    ctx = lax.axis_index("ctx")
    tp = lax.axis_index("tp")
    s, y = ctx // 2, ctx % 2
    z = 1 - y
    x, c = tp // 2, tp % 2
    sib = (2 * s + z, tp)
    down = (2 * lax.rem(s + 1, stages) + y, tp)
    up = (2 * lax.rem(s + stages - 1, stages) + y, tp)
    down_d = (2 * lax.rem(s + 1, stages) + z, tp)
    up_d = (2 * lax.rem(s + stages - 1, stages) + z, tp)
    xnb = (ctx, 2 * (1 - x) + c)
    core = (ctx, 2 * x + 1 - c)
    t_own, t_core, t_x, t_f = tp, 2 * x + 1 - c, 2 * (1 - x) + c, 2 * (1 - x) + 1 - c

    barrier = pltpu.get_barrier_semaphore()
    for dev in (sib, down, up, down_d, up_d, xnb, core):
        pl.semaphore_signal(barrier, inc=1, device_id=dev, device_id_type=MESH)

    def remote(src, dst, a, b, dev):
        return pltpu.make_async_remote_copy(
            src_ref=src, dst_ref=dst, send_sem=a, recv_sem=b, device_id=dev, device_id_type=MESH
        )

    def w_copy(t, h):
        i = PARTS * t + h
        return pltpu.make_async_copy(w_hbm.at[pl.ds(i * part, part)], wbuf.at[i], w_sem.at[i])

    def g_part(h):
        return g_in.at[:, h * part : (h + 1) * part]

    own_q = pl.ds(pl.multiple_of(y * gw, gw), gw)
    loads = [
        pltpu.make_async_copy(src, dst, in_sem.at[i])
        for i, (src, dst) in enumerate(
            [(k_hbm, k_in), (v_hbm, v_in), (seg_hbm, seg_in), (q_in.at[:, own_q], qbuf.at[y])]
            + [(g_part(h), gbuf.at[t_own, h]) for h in range(PARTS)]
        )
    ]
    for copy in loads:
        copy.start()
    for t in (t_own, t_core, t_x, t_f):
        for h in range(PARTS):
            w_copy(t, h).start()
    for copy in loads[:3]:
        copy.wait()

    def fill(dst, g):
        cols = pl.ds(pl.multiple_of(g * hs, hs), hs)
        dst[0:rows, :] = k_in[:, cols]
        dst[rows : 2 * rows, :] = v_in[:, cols]
        dst[2 * rows :, :] = jnp.broadcast_to(seg_in[...].astype(F32), (SEG_ROWS, rows)).astype(BF16)

    fill(kv.at[s, y], y)
    fill(ky, z)

    pl.semaphore_wait(barrier, 7)

    def chain(k, p):
        return remote(kv.at[k, p], kv.at[k, p], kv_s.at[k, p], kv_r.at[k, p], down)

    ky_copy = remote(ky, kv.at[s, y], misc_s.at[0], misc_r.at[0], sib)
    q_copy = remote(
        q_in.at[:, pl.ds(pl.multiple_of(z * gw, gw), gw)], qbuf.at[y], misc_s.at[1], misc_r.at[1], sib
    )
    u_copy = remote(usend, ubuf.at[y], misc_s.at[2], misc_r.at[2], sib)
    dq_copy = remote(dqs, dqr, misc_s.at[3], misc_r.at[3], sib)
    parts = range(PARTS)
    gx = [remote(g_part(h), gbuf.at[t_own, h], gx_s.at[h], gx_r.at[h], xnb) for h in parts]
    gc = [remote(g_part(h), gbuf.at[t_own, h], gc_s.at[h], gc_r.at[h], core) for h in parts]
    gf = [remote(gbuf.at[t_x, h], gbuf.at[t_x, h], gf_s.at[h], gf_r.at[h], core) for h in parts]
    last = s == stages - 1

    ky_copy.start()
    for copy in gx:
        copy.start()

    @pl.when(jnp.logical_not(last))
    def _():
        chain(s, y).start()

    for copy in gc:
        copy.start()

    def product(t, h):
        w_copy(t, h).wait()
        return dot(gbuf[t, h], wbuf[PARTS * t + h], 1, 0)

    for copy in loads[3:]:
        copy.wait()
    acc[...] = product(t_own, 0)
    for h in range(1, PARTS):
        acc[...] += product(t_own, h)

    ky_copy.wait_recv()
    q_copy.start()

    @pl.when(jnp.logical_not(last))
    def _():
        chain(s, z).start()

    for h in parts:
        gc[h].wait_recv()
        acc[...] += product(t_core, h)

    def arrive_part(k, p):
        chain(k, p).wait_recv()

        @pl.when(jnp.logical_not(last))
        def _():
            chain(k, p).start()

    def arrive(k):
        for p in range(2):
            arrive_part(k, p)

    for h in parts:
        gx[h].wait_recv()
        gf[h].start()
        if h in (0, 2):
            @pl.when(s >= 1)
            def _():
                arrive_part(s - 1, z if h else y)

        if h == PARTS - 1:
            @pl.when((s >= 2) & jnp.logical_not(last))
            def _():
                arrive(s - 2)

        acc[...] += product(t_x, h)

    mst[...] = jnp.full(mst.shape, -1e20, F32)
    lst[...] = jnp.zeros(lst.shape, F32)
    ot[...] = jnp.zeros(ot.shape, F32)
    ones[...] = jnp.zeros(ones.shape, F32)
    dq[...] = jnp.zeros(dq.shape, F32)

    def heads(ref, r):
        return ref[:, :, r * hs : (r + 1) * hs].reshape(pair, hs)

    def pieces(k):
        return kv[k, :, 0:rows, :].reshape(pair, hs), kv[k, :, rows : 2 * rows, :].reshape(pair, hs)

    def block(k):
        keys, values = pieces(k)
        begin = (s + 1) * pair - ones[0:1, :].astype(jnp.int32)
        qpos = s * pair + lax.broadcasted_iota(jnp.int32, (1, pair), 1)
        low = jnp.where(qpos < begin, 0, begin)
        kpos = k * pair + lax.broadcasted_iota(jnp.int32, (pair, pair), 0)
        return keys, values, (kpos <= qpos) & (kpos >= low)

    def scores(keys, allowed, r):
        sc = dot(keys, heads(qbuf, r), 1, 1) * (scale * LOG2E)
        return jnp.where(allowed, sc, -1e30)

    def statistics(i, carry):
        k = s - i

        @pl.when(last & (k < s - 1))
        def _():
            for p in range(2):
                chain(k, p).wait_recv()

        seg = kv[k, :, 2 * rows :, :].astype(F32).reshape(2 * SEG_ROWS, rows)
        count = jnp.sum(jnp.sum(seg, axis=0, keepdims=True), axis=1, keepdims=True) * (1.0 / SEG_ROWS)
        ones[...] += jnp.broadcast_to(count, ones.shape)
        keys, values, allowed = block(k)
        turned = values.T
        for r in range(RATIO):
            sc = scores(keys, allowed, r)
            if keep:
                kept[k, r] = sc
            old = mst[r : r + 1, :]
            new = jnp.maximum(old, jnp.max(sc, axis=0, keepdims=True))
            pr = jnp.exp2(sc - new)
            factor = jnp.exp2(old - new)
            mst[r : r + 1, :] = new
            lst[r : r + 1, :] = lst[r : r + 1, :] * factor + jnp.sum(pr, axis=0, keepdims=True)
            ot[r] = ot[r] * factor + dot(turned, pr.astype(BF16), 1, 0)
        return carry

    for h in parts:
        if h == PARTS - 1:
            q_copy.wait_recv()
            statistics(0, 0)
        gf[h].wait_recv()
        acc[...] += product(t_f, h)
    usend[...] = acc[:, pl.ds(pl.multiple_of(z * gw, gw), gw)].astype(BF16)
    u_copy.start()
    ubuf[y] = acc[:, pl.ds(pl.multiple_of(y * gw, gw), gw)].astype(BF16)

    @pl.when(jnp.logical_not(last))
    def _():
        def body(i, carry):
            arrive(s - 3 - i)
            return carry

        lax.fori_loop(0, s - 2, body, 0)

    lax.fori_loop(1, s + 1, statistics, 0)
    u_copy.wait_recv()
    for r in range(RATIO):
        wst[r : r + 1, :] = jnp.sum(heads(ubuf, r).astype(F32).T * ot[r], axis=0, keepdims=True)
    mst[...] = mst[...] + jnp.log2(lst[...])
    wst[...] = wst[...] / lst[...]

    here = pl.ds(pl.multiple_of(y * rows, rows), rows)
    there = pl.ds(pl.multiple_of(z * rows, rows), rows)

    halves = (here, there)

    def back(k, p, h):
        return remote(
            rs.at[k, p, halves[h]], ret.at[k, p, halves[h]],
            ret_s.at[k, 2 * p + h], ret_r.at[k, 2 * p + h], up,
        )

    def home(k, p, h):
        if h == 0:
            return remote(
                rs.at[k, p, here], ret.at[k, p, here], ret_s.at[k, 2 * p], ret_r.at[k, 2 * p], up
            )
        return remote(rs.at[k, p, there], retd.at[p], dia_s.at[p], dia_r.at[p], up_d)

    pieces4 = [(p, h) for p in range(2) for h in range(2)]

    fin = [remote(fins.at[p], finr.at[p], fin_s.at[p], fin_r.at[p], sib) for p in range(2)]

    def gradients(k, carry):
        if keep:
            keys, values = pieces(k)
        else:
            keys, values, allowed = block(k)
        turned = keys.T
        dk = jnp.zeros((pair, hs), F32)
        dv = jnp.zeros((pair, hs), F32)
        for r in range(RATIO):
            sc = kept[k, r] if keep else scores(keys, allowed, r)
            dp = dot(values, heads(ubuf, r), 1, 1)
            pr = jnp.exp2(sc - mst[r : r + 1, :])
            ds = (pr * (dp - wst[r : r + 1, :])).astype(BF16)
            dv += dot(pr.astype(BF16), heads(ubuf, r), 1, 0)
            dk += dot(ds, heads(qbuf, r), 1, 0)
            dq[r] += dot(turned, ds, 1, 0)
        own[k, 0] = dk * scale
        own[k, 1] = dv

        @pl.when(last & (k < s))
        def _():
            for p in range(2):
                rs[k, p] = own[k, p].astype(BF16)

        @pl.when(last & (k >= 2) & (k < s))
        def _():
            for p, h in pieces4:
                back(k - 2, p, h).wait_send()

        @pl.when(last & (k < s - 1))
        def _():
            for p, h in pieces4:
                back(k, p, h).start()

        @pl.when(last & (k == s - 1))
        def _():
            for p, h in pieces4:
                home(s - 1, p, h).start()

        return carry

    lax.fori_loop(0, s + 1, gradients, 0)

    for r in range(RATIO):
        dqs[:, r * hs : (r + 1) * hs] = (
            dq[r, :, pl.ds(pl.multiple_of(z * rows, rows), rows)] * scale
        ).T.astype(BF16)
    dq_copy.start()
    for r in range(RATIO):
        q_out[:, pl.ds(pl.multiple_of(y * gw, gw) + r * hs, hs)] = (
            dq[r, :, pl.ds(pl.multiple_of(y * rows, rows), rows)] * scale
        ).T.astype(BF16)

    for p in range(2):
        fins[p] = own[s, p, there, :]
        fin[p].start()

    @pl.when(jnp.logical_not(last))
    def _():
        def body(k, carry):
            for p in range(2):
                for h in range(2):
                    back(k, p, h).wait_recv()
                    rs[k, p, halves[h], :] = (
                        own[k, p, halves[h], :] + ret[k, p, halves[h], :].astype(F32)
                    ).astype(BF16)

                    @pl.when(k < s - 1)
                    def _():
                        back(k, p, h).start()

                    @pl.when(k == s - 1)
                    def _():
                        home(s - 1, p, h).start()

            return carry

        lax.fori_loop(0, s, body, 0)

    dq_copy.wait_recv()
    q_out[:, pl.ds(pl.multiple_of(z * gw, gw), gw)] = dqr[...]
    mine = pl.ds(pl.multiple_of(y * hs, hs), hs)
    theirs = pl.ds(pl.multiple_of(z * hs, hs), hs)
    for p, out in enumerate((k_out, v_out)):
        fin[p].wait_recv()

        @pl.when(last)
        def _():
            out[:, mine] = own[s, p, here, :].astype(BF16)
            out[:, theirs] = finr[p].astype(BF16)

        @pl.when(jnp.logical_not(last))
        def _():
            for h in range(2):
                home(s, p, h).wait_recv()
            out[:, mine] = (own[s, p, here, :] + ret[s, p, here, :].astype(F32)).astype(BF16)
            out[:, theirs] = (finr[p] + retd[p].astype(F32)).astype(BF16)

    for copy in (ky_copy, q_copy, u_copy, dq_copy, *gx, *gc, *gf, *fin):
        copy.wait_send()

    @pl.when(jnp.logical_not(last))
    def _():
        def body(k, carry):
            for p in range(2):
                chain(k, p).wait_send()
            return carry

        lax.fori_loop(0, s + 1, body, 0)

    def drain(k, carry):
        for p, h in pieces4:
            back(k, p, h).wait_send()
        return carry

    lax.fori_loop(jnp.where(last, jnp.maximum(s - 2, 0), 0), s - 1, drain, 0)

    @pl.when(s >= 1)
    def _():
        for p, h in pieces4:
            home(s - 1, p, h).wait_send()


def hand_over(a, b, c, x, y, z):
    x[...] = a[...]
    y[...] = b[...]
    z[...] = c[...]


def per_device(stages, queries, keys, values, grad_out, out_weight, segments):
    rows, wide = queries.shape
    depth = grad_out.shape[1]
    pair, hs, gw = 2 * rows, HEAD_SIZE, RATIO * HEAD_SIZE
    vmem = pl.BlockSpec(memory_space=pltpu.VMEM)
    dma = pltpu.SemaphoreType.DMA
    grads = pl.pallas_call(
        functools.partial(kernel, stages),
        out_shape=(
            jax.ShapeDtypeStruct(queries.shape, BF16),
            jax.ShapeDtypeStruct(keys.shape, BF16),
            jax.ShapeDtypeStruct(values.shape, BF16),
        ),
        in_specs=[pl.BlockSpec(memory_space=pl.ANY)] * 6,
        out_specs=(vmem, vmem, vmem),
        scratch_shapes=[
            pltpu.VMEM(keys.shape, BF16),
            pltpu.VMEM(values.shape, BF16),
            pltpu.VMEM((1, rows), jnp.int32),
            pltpu.VMEM((4 * PARTS, depth // PARTS, wide), BF16),
            pltpu.VMEM((4, PARTS, rows, depth // PARTS), BF16),
            pltpu.VMEM((rows, wide), F32),
            pltpu.VMEM((stages, 2, pair + SEG_ROWS, hs), BF16),
            pltpu.VMEM((pair + SEG_ROWS, hs), BF16),
            pltpu.VMEM((2, rows, gw), BF16),
            pltpu.VMEM((2, rows, gw), BF16),
            pltpu.VMEM((rows, gw), BF16),
            pltpu.VMEM((RATIO, pair), F32),
            pltpu.VMEM((RATIO, pair), F32),
            pltpu.VMEM((RATIO, pair), F32),
            pltpu.VMEM((8, pair), F32),
            pltpu.VMEM((RATIO, hs, pair), F32),
            pltpu.VMEM((stages if stages <= KEPT_STAGES else 1, RATIO, pair, pair), F32),
            pltpu.VMEM((RATIO, hs, pair), F32),
            pltpu.VMEM((rows, gw), BF16),
            pltpu.VMEM((rows, gw), BF16),
            pltpu.VMEM((stages, 2, pair, hs), F32),
            pltpu.VMEM((stages, 2, pair, hs), BF16),
            pltpu.VMEM((stages, 2, pair, hs), BF16),
            pltpu.VMEM((2, rows, hs), BF16),
            pltpu.VMEM((2, rows, hs), F32),
            pltpu.VMEM((2, rows, hs), F32),
            dma((4 * PARTS,)), dma((4 + PARTS,)),
            *[dma((PARTS,))] * 6,
            dma((stages, 2)), dma((stages, 2)), dma((stages, 4)), dma((stages, 4)), dma((2,)), dma((2,)),
            dma((4,)), dma((4,)), dma((2,)), dma((2,)),
        ],
        compiler_params=pltpu.CompilerParams(
            collective_id=0, has_side_effects=True, vmem_limit_bytes=56 * 1024 * 1024
        ),
        name="attention_backward",
    )(queries, keys, values, grad_out, out_weight, segments.reshape(1, rows))
    return pl.pallas_call(
        hand_over,
        out_shape=tuple(jax.ShapeDtypeStruct(a.shape, a.dtype) for a in grads),
        in_specs=[vmem] * 3,
        out_specs=(vmem,) * 3,
        compiler_params=pltpu.CompilerParams(vmem_limit_bytes=56 * 1024 * 1024),
        name="hand_over",
    )(*grads)


def solution(mesh):
    in_specs = (
        P("ctx", "tp"),
        P("ctx", "tp"),
        P("ctx", "tp"),
        P("ctx", "tp"),
        P(None, "tp"),
        P("ctx"),
    )
    out_specs = (P("ctx", "tp"), P("ctx", "tp"), P("ctx", "tp"))
    return jax.shard_map(
        functools.partial(per_device, mesh.shape["ctx"] // 2),
        mesh=mesh, in_specs=in_specs, out_specs=out_specs, check_vma=False,
    )
```

```python
import functools

import jax
import jax.numpy as jnp
from jax import lax
from jax.experimental import pallas as pl
from jax.experimental.pallas import tpu as pltpu
from jax.sharding import PartitionSpec as P

QUERY_HEADS = 32
KEY_VALUE_HEADS = 8
HEAD_SIZE = 128
RATIO = QUERY_HEADS // KEY_VALUE_HEADS
SEG_ROWS = 16
KEPT_STAGES = 8
PARTS = 4
LOG2E = 1.4426950408889634
MESH = pl.DeviceIdType.MESH
F32 = jnp.float32
BF16 = jnp.bfloat16


def dot(a, b, ca, cb):
    return lax.dot_general(a, b, (((ca,), (cb,)), ((), ())), preferred_element_type=F32)


def kernel(
    stages, q_in, k_hbm, v_hbm, g_in, w_hbm, seg_hbm,
    q_out, k_out, v_out,
    k_in, v_in, seg_in, wbuf, gbuf, acc, kv, ky, qbuf, ubuf, usend, mst, lst, wst, ones, ot, kept,
    dq, dqs, dqr, own, rs, ret, retd, fins, finr,
    w_sem, in_sem, gx_s, gx_r, gc_s, gc_r, gf_s, gf_r, kv_s, kv_r, ret_s, ret_r, dia_s, dia_r,
    misc_s, misc_r, fin_s, fin_r,
):
    rows = k_hbm.shape[0]
    pair = 2 * rows
    hs = HEAD_SIZE
    gw = RATIO * hs
    keep = stages <= KEPT_STAGES
    part = g_in.shape[1] // PARTS
    scale = HEAD_SIZE ** -0.5
    ctx = lax.axis_index("ctx")
    tp = lax.axis_index("tp")
    s, y = ctx // 2, ctx % 2
    z = 1 - y
    x, c = tp // 2, tp % 2
    sib = (2 * s + z, tp)
    down = (2 * lax.rem(s + 1, stages) + y, tp)
    up = (2 * lax.rem(s + stages - 1, stages) + y, tp)
    down_d = (2 * lax.rem(s + 1, stages) + z, tp)
    up_d = (2 * lax.rem(s + stages - 1, stages) + z, tp)
    xnb = (ctx, 2 * (1 - x) + c)
    core = (ctx, 2 * x + 1 - c)
    t_own, t_core, t_x, t_f = tp, 2 * x + 1 - c, 2 * (1 - x) + c, 2 * (1 - x) + 1 - c

    barrier = pltpu.get_barrier_semaphore()
    for dev in (sib, down, up, down_d, up_d, xnb, core):
        pl.semaphore_signal(barrier, inc=1, device_id=dev, device_id_type=MESH)

    def remote(src, dst, a, b, dev):
        return pltpu.make_async_remote_copy(
            src_ref=src, dst_ref=dst, send_sem=a, recv_sem=b, device_id=dev, device_id_type=MESH
        )

    def w_copy(t, h):
        i = PARTS * t + h
        return pltpu.make_async_copy(w_hbm.at[pl.ds(i * part, part)], wbuf.at[i], w_sem.at[i])

    def g_part(h):
        return g_in.at[:, h * part : (h + 1) * part]

    own_q = pl.ds(pl.multiple_of(y * gw, gw), gw)
    loads = [
        pltpu.make_async_copy(src, dst, in_sem.at[i])
        for i, (src, dst) in enumerate(
            [(k_hbm, k_in), (v_hbm, v_in), (seg_hbm, seg_in), (q_in.at[:, own_q], qbuf.at[y])]
            + [(g_part(h), gbuf.at[t_own, h]) for h in range(PARTS)]
        )
    ]
    for copy in loads:
        copy.start()
    for t in (t_own, t_core, t_x, t_f):
        for h in range(PARTS):
            w_copy(t, h).start()
    for copy in loads[:3]:
        copy.wait()

    def fill(dst, g):
        cols = pl.ds(pl.multiple_of(g * hs, hs), hs)
        dst[0:rows, :] = k_in[:, cols]
        dst[rows : 2 * rows, :] = v_in[:, cols]
        dst[2 * rows :, :] = jnp.broadcast_to(seg_in[...].astype(F32), (SEG_ROWS, rows)).astype(BF16)

    fill(kv.at[s, y], y)
    fill(ky, z)

    pl.semaphore_wait(barrier, 7)

    def chain(k, p):
        return remote(kv.at[k, p], kv.at[k, p], kv_s.at[k, p], kv_r.at[k, p], down)

    ky_copy = remote(ky, kv.at[s, y], misc_s.at[0], misc_r.at[0], sib)
    q_copy = remote(
        q_in.at[:, pl.ds(pl.multiple_of(z * gw, gw), gw)], qbuf.at[y], misc_s.at[1], misc_r.at[1], sib
    )
    u_copy = remote(usend, ubuf.at[y], misc_s.at[2], misc_r.at[2], sib)
    dq_copy = remote(dqs, dqr, misc_s.at[3], misc_r.at[3], sib)
    parts = range(PARTS)
    gx = [remote(g_part(h), gbuf.at[t_own, h], gx_s.at[h], gx_r.at[h], xnb) for h in parts]
    gc = [remote(g_part(h), gbuf.at[t_own, h], gc_s.at[h], gc_r.at[h], core) for h in parts]
    gf = [remote(gbuf.at[t_x, h], gbuf.at[t_x, h], gf_s.at[h], gf_r.at[h], core) for h in parts]
    last = s == stages - 1

    ky_copy.start()
    for copy in gx:
        copy.start()

    @pl.when(jnp.logical_not(last))
    def _():
        chain(s, y).start()

    for copy in gc:
        copy.start()

    def product(t, h):
        w_copy(t, h).wait()
        return dot(gbuf[t, h], wbuf[PARTS * t + h], 1, 0)

    for copy in loads[3:]:
        copy.wait()
    acc[...] = product(t_own, 0)
    for h in range(1, PARTS):
        acc[...] += product(t_own, h)

    ky_copy.wait_recv()
    q_copy.start()

    @pl.when(jnp.logical_not(last))
    def _():
        chain(s, z).start()

    for h in parts:
        gc[h].wait_recv()
        acc[...] += product(t_core, h)

    def arrive_part(k, p):
        chain(k, p).wait_recv()

        @pl.when(jnp.logical_not(last))
        def _():
            chain(k, p).start()

    def arrive(k):
        for p in range(2):
            arrive_part(k, p)

    for h in parts:
        gx[h].wait_recv()
        gf[h].start()
        if h in (0, 2):
            @pl.when(s >= 1)
            def _():
                arrive_part(s - 1, z if h else y)

        if h == PARTS - 1:
            @pl.when((s >= 2) & jnp.logical_not(last))
            def _():
                arrive(s - 2)

        acc[...] += product(t_x, h)

    mst[...] = jnp.full(mst.shape, -1e20, F32)
    lst[...] = jnp.zeros(lst.shape, F32)
    ot[...] = jnp.zeros(ot.shape, F32)
    ones[...] = jnp.zeros(ones.shape, F32)
    dq[...] = jnp.zeros(dq.shape, F32)

    def heads(ref, r):
        return ref[:, :, r * hs : (r + 1) * hs].reshape(pair, hs)

    def pieces(k):
        return kv[k, :, 0:rows, :].reshape(pair, hs), kv[k, :, rows : 2 * rows, :].reshape(pair, hs)

    def block(k):
        keys, values = pieces(k)
        begin = (s + 1) * pair - ones[0:1, :].astype(jnp.int32)
        qpos = s * pair + lax.broadcasted_iota(jnp.int32, (1, pair), 1)
        low = jnp.where(qpos < begin, 0, begin)
        kpos = k * pair + lax.broadcasted_iota(jnp.int32, (pair, pair), 0)
        return keys, values, (kpos <= qpos) & (kpos >= low)

    def scores(keys, allowed, r):
        sc = dot(keys, heads(qbuf, r), 1, 1) * (scale * LOG2E)
        return jnp.where(allowed, sc, -1e30)

    def statistics(i, carry):
        k = s - i

        @pl.when(last & (k < s - 1))
        def _():
            for p in range(2):
                chain(k, p).wait_recv()

        seg = kv[k, :, 2 * rows :, :].astype(F32).reshape(2 * SEG_ROWS, rows)
        count = jnp.sum(jnp.sum(seg, axis=0, keepdims=True), axis=1, keepdims=True) * (1.0 / SEG_ROWS)
        ones[...] += jnp.broadcast_to(count, ones.shape)
        keys, values, allowed = block(k)
        turned = values.T
        for r in range(RATIO):
            sc = scores(keys, allowed, r)
            if keep:
                kept[k, r] = sc
            old = mst[r : r + 1, :]
            new = jnp.maximum(old, jnp.max(sc, axis=0, keepdims=True))
            pr = jnp.exp2(sc - new)
            factor = jnp.exp2(old - new)
            mst[r : r + 1, :] = new
            lst[r : r + 1, :] = lst[r : r + 1, :] * factor + jnp.sum(pr, axis=0, keepdims=True)
            ot[r] = ot[r] * factor + dot(turned, pr.astype(BF16), 1, 0)
        return carry

    for h in parts:
        if h == PARTS - 1:
            q_copy.wait_recv()
            statistics(0, 0)
        gf[h].wait_recv()
        acc[...] += product(t_f, h)
    usend[...] = acc[:, pl.ds(pl.multiple_of(z * gw, gw), gw)].astype(BF16)
    u_copy.start()
    ubuf[y] = acc[:, pl.ds(pl.multiple_of(y * gw, gw), gw)].astype(BF16)

    @pl.when(jnp.logical_not(last))
    def _():
        def body(i, carry):
            arrive(s - 3 - i)
            return carry

        lax.fori_loop(0, s - 2, body, 0)

    lax.fori_loop(1, s + 1, statistics, 0)
    u_copy.wait_recv()
    for r in range(RATIO):
        wst[r : r + 1, :] = jnp.sum(heads(ubuf, r).astype(F32).T * ot[r], axis=0, keepdims=True)
    mst[...] = mst[...] + jnp.log2(lst[...])
    wst[...] = wst[...] / lst[...]

    here = pl.ds(pl.multiple_of(y * rows, rows), rows)
    there = pl.ds(pl.multiple_of(z * rows, rows), rows)

    halves = (here, there)

    def back(k, p, h):
        return remote(
            rs.at[k, p, halves[h]], ret.at[k, p, halves[h]],
            ret_s.at[k, 2 * p + h], ret_r.at[k, 2 * p + h], up,
        )

    def home(k, p, h):
        if h == 0:
            return remote(
                rs.at[k, p, here], ret.at[k, p, here], ret_s.at[k, 2 * p], ret_r.at[k, 2 * p], up
            )
        return remote(rs.at[k, p, there], retd.at[p], dia_s.at[p], dia_r.at[p], up_d)

    pieces4 = [(p, h) for p in range(2) for h in range(2)]

    fin = [remote(fins.at[p], finr.at[p], fin_s.at[p], fin_r.at[p], sib) for p in range(2)]

    def stacked(ref):
        return jnp.concatenate([heads(ref, r) for r in range(RATIO)], 0)

    def gradients(k, carry):
        if keep:
            keys, values = pieces(k)
        else:
            keys, values, allowed = block(k)
        turned = keys.T
        probs_low, dscores_low = [], []
        for r in range(RATIO):
            sc = kept[k, r] if keep else scores(keys, allowed, r)
            dp = dot(values, heads(ubuf, r), 1, 1)
            pr = jnp.exp2(sc - mst[r : r + 1, :])
            ds = (pr * (dp - wst[r : r + 1, :])).astype(BF16)
            probs_low.append(pr.astype(BF16))
            dscores_low.append(ds)
            dq[r] += dot(turned, ds, 1, 0)
        own[k, 0] = dot(jnp.concatenate(dscores_low, 1), stacked(qbuf), 1, 0) * scale
        own[k, 1] = dot(jnp.concatenate(probs_low, 1), stacked(ubuf), 1, 0)

        @pl.when(last & (k < s))
        def _():
            for p in range(2):
                rs[k, p] = own[k, p].astype(BF16)

        @pl.when(last & (k >= 2) & (k < s))
        def _():
            for p, h in pieces4:
                back(k - 2, p, h).wait_send()

        @pl.when(last & (k < s - 1))
        def _():
            for p, h in pieces4:
                back(k, p, h).start()

        @pl.when(last & (k == s - 1))
        def _():
            for p, h in pieces4:
                home(s - 1, p, h).start()

        return carry

    lax.fori_loop(0, s + 1, gradients, 0)

    for r in range(RATIO):
        dqs[:, r * hs : (r + 1) * hs] = (
            dq[r, :, pl.ds(pl.multiple_of(z * rows, rows), rows)] * scale
        ).T.astype(BF16)
    dq_copy.start()
    for r in range(RATIO):
        q_out[:, pl.ds(pl.multiple_of(y * gw, gw) + r * hs, hs)] = (
            dq[r, :, pl.ds(pl.multiple_of(y * rows, rows), rows)] * scale
        ).T.astype(BF16)

    for p in range(2):
        fins[p] = own[s, p, there, :]
        fin[p].start()

    @pl.when(jnp.logical_not(last))
    def _():
        def body(k, carry):
            for p in range(2):
                for h in range(2):
                    back(k, p, h).wait_recv()
                    rs[k, p, halves[h], :] = (
                        own[k, p, halves[h], :] + ret[k, p, halves[h], :].astype(F32)
                    ).astype(BF16)

                    @pl.when(k < s - 1)
                    def _():
                        back(k, p, h).start()

                    @pl.when(k == s - 1)
                    def _():
                        home(s - 1, p, h).start()

            return carry

        lax.fori_loop(0, s, body, 0)

    dq_copy.wait_recv()
    q_out[:, pl.ds(pl.multiple_of(z * gw, gw), gw)] = dqr[...]
    mine = pl.ds(pl.multiple_of(y * hs, hs), hs)
    theirs = pl.ds(pl.multiple_of(z * hs, hs), hs)
    for p, out in enumerate((k_out, v_out)):
        fin[p].wait_recv()

        @pl.when(last)
        def _():
            out[:, mine] = own[s, p, here, :].astype(BF16)
            out[:, theirs] = finr[p].astype(BF16)

        @pl.when(jnp.logical_not(last))
        def _():
            for h in range(2):
                home(s, p, h).wait_recv()
            out[:, mine] = (own[s, p, here, :] + ret[s, p, here, :].astype(F32)).astype(BF16)
            out[:, theirs] = (finr[p] + retd[p].astype(F32)).astype(BF16)

    for copy in (ky_copy, q_copy, u_copy, dq_copy, *gx, *gc, *gf, *fin):
        copy.wait_send()

    @pl.when(jnp.logical_not(last))
    def _():
        def body(k, carry):
            for p in range(2):
                chain(k, p).wait_send()
            return carry

        lax.fori_loop(0, s + 1, body, 0)

    def drain(k, carry):
        for p, h in pieces4:
            back(k, p, h).wait_send()
        return carry

    lax.fori_loop(jnp.where(last, jnp.maximum(s - 2, 0), 0), s - 1, drain, 0)

    @pl.when(s >= 1)
    def _():
        for p, h in pieces4:
            home(s - 1, p, h).wait_send()


def hand_over(a, b, c, x, y, z):
    x[...] = a[...]
    y[...] = b[...]
    z[...] = c[...]


def per_device(stages, queries, keys, values, grad_out, out_weight, segments):
    rows, wide = queries.shape
    depth = grad_out.shape[1]
    pair, hs, gw = 2 * rows, HEAD_SIZE, RATIO * HEAD_SIZE
    vmem = pl.BlockSpec(memory_space=pltpu.VMEM)
    dma = pltpu.SemaphoreType.DMA
    grads = pl.pallas_call(
        functools.partial(kernel, stages),
        out_shape=(
            jax.ShapeDtypeStruct(queries.shape, BF16),
            jax.ShapeDtypeStruct(keys.shape, BF16),
            jax.ShapeDtypeStruct(values.shape, BF16),
        ),
        in_specs=[pl.BlockSpec(memory_space=pl.ANY)] * 6,
        out_specs=(vmem, vmem, vmem),
        scratch_shapes=[
            pltpu.VMEM(keys.shape, BF16),
            pltpu.VMEM(values.shape, BF16),
            pltpu.VMEM((1, rows), jnp.int32),
            pltpu.VMEM((4 * PARTS, depth // PARTS, wide), BF16),
            pltpu.VMEM((4, PARTS, rows, depth // PARTS), BF16),
            pltpu.VMEM((rows, wide), F32),
            pltpu.VMEM((stages, 2, pair + SEG_ROWS, hs), BF16),
            pltpu.VMEM((pair + SEG_ROWS, hs), BF16),
            pltpu.VMEM((2, rows, gw), BF16),
            pltpu.VMEM((2, rows, gw), BF16),
            pltpu.VMEM((rows, gw), BF16),
            pltpu.VMEM((RATIO, pair), F32),
            pltpu.VMEM((RATIO, pair), F32),
            pltpu.VMEM((RATIO, pair), F32),
            pltpu.VMEM((8, pair), F32),
            pltpu.VMEM((RATIO, hs, pair), F32),
            pltpu.VMEM((stages if stages <= KEPT_STAGES else 1, RATIO, pair, pair), F32),
            pltpu.VMEM((RATIO, hs, pair), F32),
            pltpu.VMEM((rows, gw), BF16),
            pltpu.VMEM((rows, gw), BF16),
            pltpu.VMEM((stages, 2, pair, hs), F32),
            pltpu.VMEM((stages, 2, pair, hs), BF16),
            pltpu.VMEM((stages, 2, pair, hs), BF16),
            pltpu.VMEM((2, rows, hs), BF16),
            pltpu.VMEM((2, rows, hs), F32),
            pltpu.VMEM((2, rows, hs), F32),
            dma((4 * PARTS,)), dma((4 + PARTS,)),
            *[dma((PARTS,))] * 6,
            dma((stages, 2)), dma((stages, 2)), dma((stages, 4)), dma((stages, 4)), dma((2,)), dma((2,)),
            dma((4,)), dma((4,)), dma((2,)), dma((2,)),
        ],
        compiler_params=pltpu.CompilerParams(
            collective_id=0, has_side_effects=True, vmem_limit_bytes=56 * 1024 * 1024
        ),
        name="attention_backward",
    )(queries, keys, values, grad_out, out_weight, segments.reshape(1, rows))
    return pl.pallas_call(
        hand_over,
        out_shape=tuple(jax.ShapeDtypeStruct(a.shape, a.dtype) for a in grads),
        in_specs=[vmem] * 3,
        out_specs=(vmem,) * 3,
        compiler_params=pltpu.CompilerParams(vmem_limit_bytes=56 * 1024 * 1024),
        name="hand_over",
    )(*grads)


def solution(mesh):
    in_specs = (
        P("ctx", "tp"),
        P("ctx", "tp"),
        P("ctx", "tp"),
        P("ctx", "tp"),
        P(None, "tp"),
        P("ctx"),
    )
    out_specs = (P("ctx", "tp"), P("ctx", "tp"), P("ctx", "tp"))
    return jax.shard_map(
        functools.partial(per_device, mesh.shape["ctx"] // 2),
        mesh=mesh, in_specs=in_specs, out_specs=out_specs, check_vma=False,
    )
```
